32 devices in a mesh: fsdp: 4 (over z), rep: 8 (over y, x, core).
Axes of the slice: x: 2, y: 2, z: 4, core: 2. Of those that a mesh axis runs over, the one named last changes fastest.
Arguments:
- embedded: bfloat16 [2, 32, 384, 768], P(None, ('fsdp', 'rep')), may hold values from -6 to 6
- cotangent: bfloat16 [2, 32, 384, 768], P(None, ('fsdp', 'rep')), may hold values from -6 to 6
- ngram_ids: int32 [2, 2, 32, 384], P(None, None, ('fsdp', 'rep')), may hold values from 0 to 7167
- segments: int32 [2, 32, 384], P(None, ('fsdp', 'rep')), may hold values from 0 to 2, never falling along the last dimension, each value on 1 to 192 neighbouring positions
- live_mask: int32 [2, 32, 384], P(None, ('fsdp', 'rep')), may hold values from 0 to 1, as said below
- tables: bfloat16 [2, 7168, 192], P(None, 'fsdp'), may hold values from -6 to 6
- w_qkv: bfloat16 [768, 2304], P('fsdp'), may hold values from -0.21875 to 0.21875
- w_out: bfloat16 [768, 768], P('fsdp'), may hold values from -0.875 to 0.875
- w_gate_up: bfloat16 [768, 4096], P('fsdp'), may hold values from -0.21875 to 0.21875
- w_down: bfloat16 [2048, 768], P('fsdp'), may hold values from -0.125 to 0.125
- up_proj: bfloat16 [384, 768], P('fsdp'), may hold values from -0.3125 to 0.3125
- norm_gains: bfloat16 [2, 768], P(None, 'fsdp'), may hold values from 0.5 to 1.5
Outputs:
- output: bfloat16 [2, 32, 384, 768], P(None, ('fsdp', 'rep'))
- embedding_grad: bfloat16 [2, 32, 384, 768], P(None, ('fsdp', 'rep'))
- table_grad: float32 [2, 7168, 192], P(None, 'fsdp')
- qkv_grad: float32 [768, 2304], P('fsdp')
- out_grad: float32 [768, 768], P('fsdp')
- gate_up_grad: float32 [768, 4096], P('fsdp')
- down_grad: float32 [2048, 768], P('fsdp')
- up_grad: float32 [384, 768], P('fsdp')
- gains_grad: float32 [2, 768], P(None, 'fsdp')
The draws below stay inside these ranges and needn't reach their ends.
Inputs may be any that keep to these rules, and one draw needn't show every extreme that they name: `segments`: segment numbers never fall along a sequence; every sequence holds 3 documents of 1 to 192 positions, one of exactly 192. `live_mask`: in each sequence the real tokens come first and the padding last; at most 96 positions of a sequence are padding, and some sequence has exactly that many.
All inputs are finite; a program needn't handle non-finite values.
Results may differ from the reference program's by a relative error of at most 0.015.
Values may be sent and summed in bfloat16 or wider, within the bound.
No kernel may reach another device: no remote copies, remote signals or barrier semaphores. Data moves between devices by JAX's collectives and lax.ppermute only.
A program may use at most 192 MiB of HBM per device.

```python
import math
import jax
import jax.numpy as jnp
import numpy as np
from jax import lax

D = 768
HEADS = 12
HEAD_DIM = 64
FF = 2048
EMB = 192
SEQ = 384
MICRO = 2
SEQS = 32
ROWS = 7168


def draw_live_mask(key, part):
    padding = jax.random.randint(key, (MICRO, SEQS), 0, SEQ // 4 + 1, dtype=jnp.int32)
    padding = padding.at[0, 0].set(SEQ // 4)
    position_ids = jnp.arange(SEQ, dtype=jnp.int32)
    return (position_ids[None, None, :] < (SEQ - padding)[:, :, None]).astype(jnp.int32)


def plant(drawn, key, low, high):
    extent = drawn.shape
    place = [jax.random.randint(jax.random.fold_in(key, axis), (), 0, extent[axis]) for axis in range(len(extent))]
    drawn = drawn.at[tuple(place)].set(low)
    longest = extent.index(max(extent))
    place[longest] = (place[longest] + 1) % extent[longest]
    return drawn.at[tuple(place)].set(high)


def levels(rng, extent, shards, least, top_value):
    gain = 1.0
    for dim, parts in shards:
        steps = jax.random.uniform(jax.random.fold_in(jax.random.fold_in(rng, 6), dim), (parts,), jnp.float32, least / len(shards), top_value / len(shards))
        gain = gain * jnp.repeat(jnp.exp(steps), extent[dim] // parts).reshape((-1,) + (1,) * (len(extent) - 1 - dim))
    return gain


def rank_table(number_of, lean):
    portions = [(1 << 20) // math.isqrt(rank ** lean) + 1 for rank in range(1, number_of + 1)]
    spread = 1 + sum(portions) // (1 << 30)
    return np.cumsum(np.array([max(1, weight // spread) for weight in portions]))


def skewed_ids(stream_key, shape, amount, skew):
    grid = rank_table(amount, skew)
    pick = jax.random.randint(jax.random.fold_in(stream_key, 1), shape, 0, int(grid[amount - 1]))
    grade = jnp.searchsorted(jnp.asarray(grid, jnp.int32), pick, side="right")
    return jax.random.permutation(jax.random.fold_in(stream_key, 2), amount)[grade].astype(jnp.int32)


def profile(count, total, most, slope):
    portions = [(1 << 20) // math.isqrt(grade ** slope) + 1 for grade in range(2, count + 1)]
    spare, counts = total - most - (count - 1), [1] * (count - 1)
    while spare > 0:
        movable = [i for i in range(count - 1) if counts[i] < most]
        mass, remaining = sum([portions[i] for i in movable]), spare
        for i in movable:
            extra = min(most - counts[i], max(1, remaining * portions[i] // mass), spare)
            counts[i] = counts[i] + extra
            spare = spare - extra
    return np.array([most] + counts)


def uneven_parts(key, number_of, total, reach, slope):
    if number_of == 2:
        one = jax.random.randint(key, (), max(1, total - reach), min(reach, total - 1) + 1)
        return jnp.stack([one, total - one])
    sizes = jnp.asarray(profile(number_of, total, reach, slope), jnp.int32)
    twos = (number_of - 1) // 2
    giver, sink = sizes[1:1 + 2 * twos:2], sizes[2:2 + 2 * twos:2]
    margin = jnp.minimum(giver - 1, reach - sink)
    passed = jax.random.randint(jax.random.fold_in(key, 1), (twos,), 0, 1 << 20) % (margin + 1)
    sizes = sizes.at[1:1 + 2 * twos:2].set(giver - passed).at[2:2 + 2 * twos:2].set(sink + passed)
    return sizes[jax.random.permutation(jax.random.fold_in(key, 2), number_of)]


def normal_values(stream_key, dims, width, reach, shards=(), kind=jnp.bfloat16):
    values = width * jax.random.normal(stream_key, dims, jnp.float32)
    if shards:
        values = values * levels(stream_key, dims, shards, -0.22, 0.18)
    return jnp.clip(values, -reach, reach).astype(kind)


def setup_inputs(seed: int = 0) -> dict:
    streams_of = jax.random.split(jax.random.key(seed), 13)
    embedded = normal_values(streams_of[0], (MICRO, SEQS, SEQ, D), 1.0, 6.0, ((1, 32),))
    cotangent = normal_values(streams_of[1], (MICRO, SEQS, SEQ, D), 1.0, 6.0, ((1, 32),))
    ngram_ids = plant(skewed_ids(streams_of[2], (2, MICRO, SEQS, SEQ), ROWS, 2), jax.random.fold_in(streams_of[2], 3), 0, ROWS - 1).astype(jnp.int32)
    segments = jax.vmap(lambda own: jnp.searchsorted(jnp.cumsum(uneven_parts(own, 3, SEQ, SEQ // 2, 0)), jnp.arange(SEQ), side="right"))(jax.random.split(streams_of[3], MICRO * SEQS)).reshape((MICRO, SEQS, SEQ)).astype(jnp.int32)
    live_mask = draw_live_mask(jax.random.fold_in(streams_of[12], 71), 0)
    tables = normal_values(streams_of[5], (2, ROWS, EMB), 1.0, 6.0, ((1, 4),))
    w_qkv = normal_values(streams_of[6], (D, 3 * D), D ** -0.5, 0.21875, ((0, 4),))
    w_out = normal_values(streams_of[7], (D, D), (D // 16) ** -0.5, 0.875, ((0, 4),))
    w_gate_up = normal_values(streams_of[8], (D, 2 * FF), D ** -0.5, 0.21875, ((0, 4),))
    w_down = normal_values(streams_of[9], (FF, D), FF ** -0.5, 0.125, ((0, 4),))
    up_proj = normal_values(streams_of[10], (2 * EMB, D), (2 * EMB) ** -0.5, 0.3125, ((0, 4),))
    norm_gains = jnp.clip(1.0 + 0.1 * jax.random.normal(streams_of[11], (2, D), jnp.float32), 0.5, 1.5).astype(jnp.bfloat16)
    return {"embedded": embedded, "cotangent": cotangent, "ngram_ids": ngram_ids, "segments": segments, "live_mask": live_mask, "tables": tables, "w_qkv": w_qkv, "w_out": w_out, "w_gate_up": w_gate_up, "w_down": w_down, "up_proj": up_proj, "norm_gains": norm_gains}


@jax.custom_vjp
def low(v):
    return lax.optimization_barrier(v.astype(jnp.bfloat16)).astype(jnp.float32)

@jax.custom_vjp
def low_back(v):
    return v

def low_keep(v):
    return (low(v), None)

def low_pass(kept, grad):
    return (grad,)

def back_keep(v):
    return (v, None)

def back_low(kept, grad):
    return (low(grad),)
low.defvjp(low_keep, low_pass)
low_back.defvjp(back_keep, back_low)
highest = lax.Precision.HIGHEST
norm_eps = 1e-05
theta_base = 10000.0
masked_score = -1e+30

def matmul(left, right):
    return jnp.dot(left, right, precision=highest)

def rotary_tables(segment, head_dim):
    seq_len = segment.shape[0]
    position_ids = jnp.arange(seq_len, dtype=jnp.int32)
    boundary = jnp.concatenate([jnp.ones((1,), dtype=bool), segment[1:] != segment[:-1]])
    starts = lax.cummax(jnp.where(boundary, position_ids, 0), axis=0)
    offsets = (position_ids - starts).astype(jnp.float32)
    half_dim = head_dim // 2
    frequency = theta_base ** (-jnp.arange(half_dim, dtype=jnp.float32) / half_dim)
    angles = offsets[:, None] * frequency[None, :]
    return (jnp.cos(angles), jnp.sin(angles))

def rotate(stacked, cosine_table, sine_table):
    half_dim = stacked.shape[-1] // 2
    low_half = stacked[..., :half_dim]
    high_half = stacked[..., half_dim:]
    cosine_table = cosine_table[:, None, :]
    sine_table = sine_table[:, None, :]
    return jnp.concatenate([low_half * cosine_table - high_half * sine_table, high_half * cosine_table + low_half * sine_table], axis=-1)

def usable_keys(segment, live_row):
    seq_len = segment.shape[0]
    position_ids = jnp.arange(seq_len, dtype=jnp.int32)
    same_doc = segment[:, None] == segment[None, :]
    causal = position_ids[None, :] <= position_ids[:, None]
    diagonal = position_ids[None, :] == position_ids[:, None]
    return same_doc & causal & (live_row[None, :] == 1) | diagonal

def rms_scale(values_in, gain_row):
    inverse = lax.rsqrt(lax.optimization_barrier(jnp.mean(values_in * values_in, axis=-1, keepdims=True)) + norm_eps)
    return values_in * inverse * gain_row

def block_layer(embedded, params, ngram_row_ids, segment, live_row):
    tables, w_qkv, w_out, w_gate_up, w_down, up_proj, norm_gains = params
    seq_len = embedded.shape[0]
    gram_rows = low_back(jnp.concatenate([tables[0][ngram_row_ids[0]], tables[1][ngram_row_ids[1]]], axis=-1))
    gram_sum = low_back(matmul(gram_rows, up_proj))
    residual = embedded + gram_sum
    act_one = low(rms_scale(residual, norm_gains[0]))
    projected = low_back(matmul(act_one, w_qkv))
    cosine_table, sine_table = rotary_tables(segment, HEAD_DIM)
    queries = low(rotate(projected[:, :D].reshape(seq_len, HEADS, HEAD_DIM), cosine_table, sine_table))
    key_rows = low(rotate(projected[:, D:2 * D].reshape(seq_len, HEADS, HEAD_DIM), cosine_table, sine_table))
    values = low(projected[:, 2 * D:].reshape(seq_len, HEADS, HEAD_DIM))
    scores = low_back(jnp.einsum('qhd,khd->hqk', queries, key_rows, precision=highest) * 0.125)
    scores = jnp.where(usable_keys(segment, live_row)[None], scores, masked_score)
    row_max = lax.optimization_barrier(jnp.max(scores, axis=-1, keepdims=True))
    exp_scores = jnp.exp(scores - row_max)
    probability = exp_scores / lax.optimization_barrier(jnp.sum(exp_scores, axis=-1, keepdims=True))
    attended = jnp.einsum('hqk,khd->qhd', low(probability), values, precision=highest).reshape(seq_len, D)
    attended = low_back(low(attended))
    residual_mid = residual + low_back(matmul(attended, w_out))
    act_two = low(rms_scale(residual_mid, norm_gains[1]))
    gate_up = low_back(matmul(act_two, w_gate_up))
    gate_part = gate_up[:, :FF]
    inner_act = low(gate_part * jax.nn.sigmoid(gate_part) * gate_up[:, FF:])
    return residual_mid + low_back(matmul(inner_act, w_down))

def reference(embedded, cotangent, ngram_ids, segments, live_mask, tables, w_qkv, w_out, w_gate_up, w_down, up_proj, norm_gains):
    seq_total = MICRO * SEQS
    block_seqs = math.gcd(seq_total, max(1, 4096 // SEQ))
    block_count = seq_total // block_seqs
    emb_blocks = embedded.reshape(block_count, block_seqs, SEQ, D)
    cot_blocks = cotangent.reshape(block_count, block_seqs, SEQ, D)
    id_blocks = jnp.moveaxis(ngram_ids, 0, 2).reshape(block_count, block_seqs, 2, SEQ)
    seg_blocks = segments.reshape(block_count, block_seqs, SEQ)
    live_blocks = live_mask.reshape(block_count, block_seqs, SEQ)
    params = tuple((weight.astype(jnp.float32) for weight in (tables, w_qkv, w_out, w_gate_up, w_down, up_proj, norm_gains)))

    def one_block(totals, inputs):
        emb_block, cot_block, id_block, seg_block, live_block = inputs

        def batched(emb_values, param_values):

            def single(emb_row, id_row, seg_row, live_row):
                return block_layer(emb_row, param_values, id_row, seg_row, live_row)
            return jax.vmap(single)(emb_values, id_block, seg_block, live_block)
        outputs, pullback = jax.vjp(batched, emb_block.astype(jnp.float32), params)
        emb_grad, param_grads = pullback(cot_block.astype(jnp.float32))
        totals = jax.tree.map(jnp.add, totals, param_grads)
        return (totals, (outputs.astype(jnp.bfloat16), emb_grad.astype(jnp.bfloat16)))
    zero_grads = jax.tree.map(jnp.zeros_like, params)
    totals, (outputs, emb_grads) = lax.scan(one_block, zero_grads, (emb_blocks, cot_blocks, id_blocks, seg_blocks, live_blocks))
    output = outputs.reshape(MICRO, SEQS, SEQ, D)
    embedding_grad = emb_grads.reshape(MICRO, SEQS, SEQ, D)
    return (output, embedding_grad, totals[0], totals[1], totals[2], totals[3], totals[4], totals[5], totals[6])
```

```python
import jax
import jax.numpy as jnp
import numpy as np
from jax import lax
from jax.experimental import pallas as pl
from jax.experimental.pallas import tpu as pltpu
from jax.sharding import Mesh, PartitionSpec as P

BF16 = jnp.bfloat16
F32 = jnp.float32
HEADS = 12
HEAD_DIM = 64
norm_eps = 1e-05
theta_base = 10000.0
masked_score = -1e30
MIB = 1 << 20

NN = (((1,), (0,)), ((), ()))
NT = (((1,), (1,)), ((), ()))
TN = (((0,), (0,)), ((), ()))


def mm(left, right, dims=NN):
    return lax.dot_general(left, right, dims, preferred_element_type=F32)


def full(shape):
    return pl.BlockSpec(shape, lambda *_: (0,) * len(shape))


def kernel_call(
    kernel, coords, args, in_specs, out_shape, out_specs, grid, scratch=(), flops=0, vmem=48, name=None
):
    moved = sum(a.size * a.dtype.itemsize for a in args)
    moved += sum(int(np.prod(s.shape)) * s.dtype.itemsize for s in out_shape)
    return pl.pallas_call(
        kernel,
        out_shape=out_shape,
        grid_spec=pltpu.PrefetchScalarGridSpec(
            num_scalar_prefetch=1,
            grid=grid,
            in_specs=in_specs,
            out_specs=out_specs,
            scratch_shapes=list(scratch),
        ),
        compiler_params=pltpu.CompilerParams(vmem_limit_bytes=vmem * MIB),
        cost_estimate=pl.CostEstimate(flops=int(flops), bytes_accessed=int(moved), transcendentals=0),
        name=name,
    )(coords, *args)


def by_core(value):
    return lax.ppermute(value, "oct", [(i, i ^ 1) for i in range(8)])


def by_x(value):
    return lax.ppermute(value, "oct", [(i, i ^ 2) for i in range(8)])


def by_y(value):
    return lax.ppermute(value, "oct", [(i, i ^ 4) for i in range(8)])


def from_ahead(value, step, size):
    return lax.ppermute(value, "fsdp", [((i + step) % size, i) for i in range(size)])


def to_ahead(value, step, size):
    return lax.ppermute(value, "fsdp", [(i, (i + step) % size) for i in range(size)])


def gather_plane(piece, depth, axis, cut):
    held = jnp.stack([from_ahead(piece, step, depth) for step in range(1, depth)])
    from_x = by_x(held)
    from_y = by_y(held)
    low = by_y(lax.slice_in_dim(from_x, 0, cut, axis=axis))
    high = by_x(lax.slice_in_dim(from_y, cut, held.shape[axis], axis=axis))
    return held, from_x, from_y, low, high


def add_low(left, right):
    return (left.astype(F32) + right.astype(F32)).astype(BF16)


def reduce_all(parts, depth):
    half = depth // 2
    kept = add_low(parts[0], by_core(parts[1]))
    a_part, b_part = kept[:, :half], kept[:, half:]
    a_part = add_low(a_part[0::2], by_x(a_part[1::2]))
    b_part = add_low(b_part[:2], by_y(b_part[2:]))
    a_part = add_low(a_part[0], by_y(a_part[1]))
    b_part = add_low(b_part[0], by_x(b_part[1]))
    return over_depth([a_part[i] for i in range(half)] + [b_part[i] for i in range(depth - half)], depth)


def over_depth(shards, depth):
    total = shards[0].astype(F32)
    for step in range(1, depth):
        total = total + to_ahead(shards[step], step, depth).astype(F32)
    return total


def over_groups(value, groups):
    if groups > 1:
        value = lax.psum(value, "grp")
    return value


def spread(value, octet, send_core=True):
    def pair(mine, other, bit):
        first = bit == 0
        return jnp.stack([jnp.where(first, mine, other), jnp.where(first, other, mine)])

    value = pair(value, by_x(value), (octet >> 1) & 1)
    value = pair(value, by_y(value), octet >> 2)
    value = pair(value, by_core(value), octet & 1)
    return value


def swap_halves(values):
    lane = lax.broadcasted_iota(jnp.int32, values.shape, 1)
    return jnp.where((lane & 63) < 32, pltpu.roll(values, 96, 1), pltpu.roll(values, 32, 1))


def project_kernel(
    coords, rows_own, rows_other, embedded, up_own, gain, qkv_own, out_own,
    a0, ax, ay, al, ah, c0, cx, cy, cl, ch,
    b0, bx, by, bl, bh, d0, dx, dy, dl, dh,
    cosine, sine,
    residual, queries, keys, values, w_qkv, w_out, w_up,
):
    depth_at, plane_at, core_at = coords[0], coords[1], coords[2]

    @pl.when(pl.program_id(0) == 0)
    def _():
        w_up[pl.ds(pl.multiple_of(depth_at * 96, 32), 96), :] = up_own[...]
        base = pl.multiple_of(depth_at * 192, 64)
        w_qkv[0, pl.ds(base, 192), :] = qkv_own[:, 0:1152]
        w_qkv[1, pl.ds(base, 192), :] = qkv_own[:, 1152:2304]
        w_out[pl.ds(base, 192), :] = out_own[...]
        groups = (
            (core_at, (a0, ax, ay, al, ah), (b0, bx, by, bl, bh)),
            (1 - core_at, (c0, cx, cy, cl, ch), (d0, dx, dy, dl, dh)),
        )
        for index, (core, tops, lows) in enumerate(groups):
            up_at = 224 if index == 0 else 0
            up_high = 96 if index == 0 else 0
            column = pl.multiple_of(core * 384, 128)
            for far in range(4):
                plane = plane_at ^ far
                for step in range(1, 4):
                    shard = (depth_at + step) % 4
                    row = pl.multiple_of(shard * 192 + plane * 48, 16)
                    at = step - 1
                    if far < 3:
                        block = lows[far][at]
                        w_qkv[core, pl.ds(row, 48), :] = block[:, 0:1152]
                        w_out[pl.ds(row, 48), pl.ds(column, 384)] = block[:, 1152:1536]
                    else:
                        w_qkv[core, pl.ds(row, 48), 0:768] = lows[3][at]
                        w_qkv[core, pl.ds(row, 48), 768:1152] = lows[4][at, :, 0:384]
                        w_out[pl.ds(row, 48), pl.ds(column, 384)] = lows[4][at, :, 384:768]

                    @pl.when(plane < 3)
                    def _():
                        up_row = pl.multiple_of(shard * 96 + plane * 32, 32)
                        if far < 3:
                            w_up[pl.ds(up_row, 32), pl.ds(column, 384)] = tops[far][at, up_at : up_at + 32, :]
                        else:
                            w_up[pl.ds(up_row, 32), pl.ds(column, 384)] = tops[4][at, up_high : up_high + 32, :]

    first = pl.multiple_of(core_at * 192, 64)
    second = pl.multiple_of(192 - core_at * 192, 64)
    total = embedded[...].astype(F32)
    total += mm(rows_own[...], w_up[pl.ds(first, 192), :])
    total += mm(rows_other[...], w_up[pl.ds(second, 192), :])
    residual[...] = total
    inverse = lax.rsqrt(jnp.mean(total * total, axis=-1, keepdims=True) + norm_eps)
    act = (total * inverse * gain[...]).astype(BF16)
    left = mm(act, w_qkv[0])
    right = mm(act, w_qkv[1])
    cos, sin = cosine[...], sine[...]
    for at in range(6):
        part = left[:, 128 * at : 128 * at + 128]
        turned = part * cos + swap_halves(part) * sin
        queries[:, 128 * at : 128 * at + 128] = (turned * 0.125).astype(BF16)
    for at in range(6):
        part = left[:, 768 + 128 * at : 896 + 128 * at] if at < 3 else right[:, 128 * at - 384 : 128 * at - 256]
        turned = part * cos + swap_halves(part) * sin
        keys[:, 128 * at : 128 * at + 128] = turned.astype(BF16)
    values[...] = right[:, 384:1152].astype(BF16)


def attend_kernel(
    coords, queries, keys, values, bias, residual, w_out, gain,
    attended, weights_out, middle, act_two, total,
):
    pair = pl.program_id(1)
    lane = lax.broadcasted_iota(jnp.int32, queries.shape, 1)
    q, k = queries[...], keys[...]
    v_t = jnp.transpose(values[...])
    outs = []
    for head in range(2):
        q_head = jnp.where((lane >= 64) == (head == 1), q, jnp.zeros_like(q))
        scores = mm(k, q_head, NT) + bias[0]
        top = jnp.max(scores, axis=0, keepdims=True)
        raised = jnp.exp(scores - top)
        weight = (raised * (1.0 / jnp.sum(raised, axis=0, keepdims=True))).astype(BF16)
        weights_out[0, 0, head] = weight
        outs.append(mm(v_t[64 * head : 64 * head + 64, :], weight))
    low = jnp.transpose(jnp.concatenate(outs, axis=0).astype(BF16))
    attended[...] = low
    part = mm(low, w_out[...])

    @pl.when(pair == 0)
    def _():
        total[...] = residual[...] + part

    @pl.when(pair > 0)
    def _():
        total[...] += part

    @pl.when(pair == 5)
    def _():
        mid = total[...]
        middle[...] = mid
        inverse = lax.rsqrt(jnp.mean(mid * mid, axis=-1, keepdims=True) + norm_eps)
        act_two[...] = (mid * inverse * gain[...]).astype(BF16)


def forward_kernel(
    coords, act, cotangent, middle, gain, w_gate, w_up, w_down,
    output, grads, grad_mid, grad_low, gain_grad, total, grad_act, act_t,
):
    at = pl.program_id(0)
    depth_at = coords[0]

    @pl.when(at == 0)
    def _():
        act_t[...] = jnp.transpose(act[...])

    a, c = act[...], cotangent[...]
    gate = mm(a, w_gate[...])
    up = mm(a, w_up[...])
    back = mm(c, w_down[...], NT)
    sig = 1.0 / (1.0 + jnp.exp(-gate))
    silu = gate * sig
    inner = (silu * up).astype(BF16)
    d_up = (back * silu).astype(BF16)
    d_gate = (back * up * (sig * (1.0 + gate * (1.0 - sig)))).astype(BF16)
    out_part = mm(inner, w_down[...])
    act_part = mm(d_gate, w_gate[...], NT) + mm(d_up, w_up[...], NT)

    @pl.when(at == 0)
    def _():
        total[...] = out_part
        grad_act[...] = act_part

    @pl.when(at > 0)
    def _():
        total[...] += out_part
        grad_act[...] += act_part

    down = mm(inner, c, TN).astype(BF16)
    gate_g = mm(act_t[...], d_gate).astype(BF16)
    up_g = mm(act_t[...], d_up).astype(BF16)
    for shard in range(4):
        far = (shard + 4 - depth_at) % 4
        grads[at, far, 0:192, :] = gate_g[192 * shard : 192 * shard + 192, :]
        grads[at + 4, far, 0:192, :] = up_g[192 * shard : 192 * shard + 192, :]
    far = (at + 4 - depth_at) % 4
    for q in range(8):
        grads[q, far, 192:256, :] = down[64 * q : 64 * q + 64, 0:512]
        grads[q, far, 256:288, 0:256] = down[64 * q : 64 * q + 32, 512:768]
        grads[q, far, 256:288, 256:512] = down[64 * q + 32 : 64 * q + 64, 512:768]

    @pl.when(at == 3)
    def _():
        mid = middle[...]
        output[...] = (mid + total[...]).astype(BF16)
        inverse = lax.rsqrt(jnp.mean(mid * mid, axis=-1, keepdims=True) + norm_eps)
        normed = mid * inverse
        grad = grad_act[...]
        gain_grad[...] = jnp.sum(grad * normed, axis=0, keepdims=True)
        n = grad * gain[...]
        g = c.astype(F32) + inverse * (n - normed * jnp.mean(n * normed, axis=-1, keepdims=True))
        grad_mid[...] = g
        grad_low[...] = g.astype(BF16)


def attend_back_kernel(
    coords, queries, keys, values, weights_in, grad_low, w_out, cosine, sine, grad_projected
):
    lane = lax.broadcasted_iota(jnp.int32, (384, 128), 1)
    grad_attended = mm(grad_low[...], w_out[...], NT).astype(BF16)
    for seq in range(2):
        rows = slice(384 * seq, 384 * seq + 384)
        q, k, v, ga = queries[rows, :], keys[rows, :], values[rows, :], grad_attended[rows, :]
        k_t = jnp.transpose(k)
        grad_k = jnp.zeros((384, 128), F32)
        grad_v = jnp.zeros((384, 128), F32)
        grad_q_t = []
        for head in range(2):
            mine = (lane >= 64) == (head == 1)
            ga_head = jnp.where(mine, ga, jnp.zeros_like(ga))
            q_head = jnp.where(mine, q, jnp.zeros_like(q))
            weight_low = weights_in[seq, 0, head]
            weight = weight_low.astype(F32)
            grad_weight = mm(v, ga_head, NT)
            row = jnp.sum(grad_weight * weight, axis=0, keepdims=True)
            grad_scores = (weight * (grad_weight - row)).astype(BF16)
            grad_v += mm(weight_low, ga_head)
            grad_k += mm(grad_scores, q_head)
            grad_q_t.append(mm(k_t[64 * head : 64 * head + 64, :], grad_scores))
        grad_q = jnp.transpose(jnp.concatenate(grad_q_t, axis=0)) * 0.125
        cos, sin = cosine[rows, :], sine[rows, :]
        grad_projected[0, rows, :] = (grad_q * cos - swap_halves(grad_q) * sin).astype(BF16)
        grad_projected[1, rows, :] = (grad_k * cos - swap_halves(grad_k) * sin).astype(BF16)
        grad_projected[2, rows, :] = grad_v.astype(BF16)


def embed_back_kernel(
    coords, grad_projected, w_qkv, w_up, residual, grad_mid, gain,
    embedding_grad, grad_rows, act, gain_grad,
):
    core_at = coords[2]
    dq, dk, dv = grad_projected[0], grad_projected[1], grad_projected[2]
    grad = mm(dq, w_qkv[0, :, 0:768], NT)
    grad += mm(dk[:, 0:384], w_qkv[0, :, 768:1152], NT)
    grad += mm(dk[:, 384:768], w_qkv[1, :, 0:384], NT)
    grad += mm(dv, w_qkv[1, :, 384:1152], NT)
    total = residual[...]
    inverse = lax.rsqrt(jnp.mean(total * total, axis=-1, keepdims=True) + norm_eps)
    normed = total * inverse
    act[...] = (normed * gain[...]).astype(BF16)
    part = jnp.sum(grad * normed, axis=0, keepdims=True)
    n = grad * gain[...]
    g = grad_mid[...] + inverse * (n - normed * jnp.mean(n * normed, axis=-1, keepdims=True))
    low = g.astype(BF16)
    embedding_grad[...] = low
    rows = mm(low, w_up[...], NT).astype(BF16)

    @pl.when(pl.program_id(0) == 0)
    def _():
        gain_grad[...] = part
        grad_rows[0, :, 0:192] = rows[:, 0:192]
        grad_rows[1, :, 0:192] = rows[:, 192:384]

    @pl.when(pl.program_id(0) == 1)
    def _():
        gain_grad[...] += part
        grad_rows[0, :, 192:384] = rows[:, 0:192]
        grad_rows[1, :, 192:384] = rows[:, 192:384]


def weight_grad_kernel(
    coords, act, grad_projected, attended, grad_low, rows_own, rows_other, embedding_grad, gains,
    grads, act_t, attended_t,
):
    depth_at, plane_at, core_at = coords[0], coords[1], coords[2]
    at = pl.program_id(0)

    @pl.when(at == 0)
    def _():
        act_t[...] = jnp.transpose(act[...])
        attended_t[...] = jnp.transpose(attended[...])

    def place(core, column, block):
        for plane in range(4):
            for shard in range(4):
                row = 192 * shard + 48 * plane
                grads[core ^ core_at, plane ^ plane_at, (shard + 4 - depth_at) % 4, 0:48, column] = block[
                    row : row + 48, :
                ]

    for step in range(6):
        @pl.when(at == step)
        def _():
            block = mm(act_t[...], grad_projected[0]).astype(BF16)
            start = 384 * (step % 3)
            place(step // 3, slice(start, start + 384), block)

    for step in range(2):
        @pl.when(at == 6 + step)
        def _():
            block = mm(attended_t[...], grad_low[:, 384 * step : 384 * step + 384]).astype(BF16)
            place(step, slice(1152, 1536), block)

    @pl.when(at == 8)
    def _():
        low = embedding_grad[...]
        mine = mm(rows_own[...], low, TN)
        other = mm(rows_other[...], low, TN)
        first = jnp.where(core_at == 0, mine, other)
        second = jnp.where(core_at == 0, other, mine)
        both = jnp.concatenate([first, second], axis=0)
        ones = gains[...]
        for core in range(2):
            for plane in range(4):
                for shard in range(4):
                    row = 96 * shard + 24 * plane
                    block = both[row : row + 24, 384 * core : 384 * core + 384]
                    extra = jnp.zeros((8, 384), F32)
                    if core == 0 and plane == 0:
                        line = jnp.concatenate(
                            [ones[0:1, 192 * shard : 192 * shard + 192], ones[1:2, 192 * shard : 192 * shard + 192]],
                            axis=1,
                        )
                        extra = jnp.concatenate([line, jnp.zeros((7, 384), F32)], axis=0)
                    block = jnp.concatenate([block, extra], axis=0).astype(BF16)
                    place_at = (core ^ core_at, plane ^ plane_at, (shard + 4 - depth_at) % 4)
                    grads[place_at[0], place_at[1], place_at[2], 48:64, 0:384] = block[0:16]
                    grads[place_at[0], place_at[1], place_at[2], 48:64, 384:768] = block[16:32]
                    grads[place_at[0], place_at[1], place_at[2], 48:64, 768:1536] = jnp.zeros((16, 768), BF16)


def table_kernel(coords, ids, own, from_x, from_y, low, high, sums, total):
    at = pl.program_id(0)

    def add(pairs):
        rows = jnp.concatenate([pairs[:, 0:192], pairs[:, 192:384]], axis=0)
        line = lax.broadcasted_iota(jnp.int32, (1792, 768), 0)
        hot = jnp.where(line == ids[0], 1.0, 0.0).astype(BF16)
        part = mm(hot, rows)

        @pl.when(at == 0)
        def _():
            total[...] = part

        @pl.when(at > 0)
        def _():
            total[...] += part

    for plane, source in enumerate((own, from_x, from_y)):
        for core in range(2):
            @pl.when(at == 2 * plane + core)
            def _():
                add(source[core])

    @pl.when(at == 6)
    def _():
        add(low[...].reshape(384, 384))

    @pl.when(at == 7)
    def _():
        add(high[...].reshape(384, 384))
        for shard in range(4):
            sums[shard, :, 0:192] = total[448 * shard : 448 * shard + 224, :].astype(BF16)
            sums[shard, :, 192:384] = total[448 * shard + 224 : 448 * shard + 448, :].astype(BF16)


def rotary_lanes(segments):
    seq_len = segments.shape[-1]
    position = jnp.arange(seq_len, dtype=jnp.int32)
    same = segments[:, :, None] == segments[:, None, :]
    start = jnp.min(jnp.where(same, position[None, None, :], seq_len), axis=-1)
    offset = (position[None, :] - start).astype(F32)
    half = HEAD_DIM // 2
    frequency = theta_base ** (-jnp.arange(half, dtype=F32) / half)
    angle = offset[..., None] * frequency
    cos, sin = jnp.cos(angle), jnp.sin(angle)
    cosine = jnp.concatenate([cos, cos, cos, cos], axis=-1)
    sine = jnp.concatenate([-sin, sin, -sin, sin], axis=-1)
    return cosine.reshape(-1, 128), sine.reshape(-1, 128), same


def sds(shape, dtype):
    return jax.ShapeDtypeStruct(shape, dtype)


def body(sizes, embedded, cotangent, ngram_ids, segments, live_mask, tables, w_qkv, w_out, w_gate_up, w_down, up_proj, norm_gains):
    depth, groups = sizes
    micro, _, seq, width = embedded.shape
    tokens = micro * seq
    rows_dev = tables.shape[1]
    depth_at = lax.axis_index("fsdp")
    octet = lax.axis_index("oct")
    core_at = octet & 1
    plane_at = octet >> 1
    coords = jnp.stack([depth_at, plane_at, core_at]).astype(jnp.int32)
    embedded = embedded.reshape(tokens, width)
    cotangent = cotangent.reshape(tokens, width)
    segments = segments.reshape(micro, seq)
    live_mask = live_mask.reshape(micro, seq)
    ids = ngram_ids.reshape(2, tokens)

    gate_rows = w_gate_up.shape[0] // 8
    down_rows = w_down.shape[0] // 8
    ff_gate_up = lax.all_gather(
        lax.dynamic_slice_in_dim(w_gate_up, octet * gate_rows, gate_rows, axis=0), ("fsdp", "oct"), axis=0, tiled=True
    )
    ff_down = lax.all_gather(
        lax.dynamic_slice_in_dim(w_down, octet * down_rows, down_rows, axis=0), ("fsdp", "oct"), axis=0, tiled=True
    )

    share = rows_dev // 4
    pairs = share // 2
    own_table = lax.dynamic_index_in_dim(tables, core_at, axis=0, keepdims=False).reshape(4, 2, pairs, 192)
    own_pairs = jnp.concatenate([own_table[:, 0], own_table[:, 1]], axis=-1)
    top = jnp.concatenate(
        [
            lax.dynamic_index_in_dim(own_pairs, plane_at, axis=0, keepdims=False),
            lax.dynamic_slice(up_proj, (jnp.minimum(plane_at, 2) * 32, core_at * 384), (32, 384)),
            jnp.pad(norm_gains, ((0, 6), (0, 192))),
        ],
        axis=0,
    )
    low = jnp.concatenate(
        [
            lax.dynamic_slice(w_qkv, (plane_at * 48, core_at * 1152), (48, 1152)),
            lax.dynamic_slice(w_out, (plane_at * 48, core_at * 384), (48, 384)),
        ],
        axis=1,
    )
    tops = gather_plane(top, depth, 1, 128)
    lows = gather_plane(low, depth, 2, 768)
    tops_other = [by_core(piece[:, 224:256] if i < 3 else (piece[:, 0:8] if i == 3 else piece[:, 96:128])) for i, piece in enumerate(tops)]
    lows_other = [by_core(piece) for piece in lows]

    gains_rel = jnp.concatenate([norm_gains[None], tops[0][:, 256:258, 0:192]], axis=0)
    gains = jnp.roll(gains_rel, depth_at, axis=0).transpose(1, 0, 2).reshape(2, width).astype(F32)
    gain_one, gain_two = gains[0:1], gains[1:2]

    ids_other = by_core(ids)
    wanted = jnp.stack(
        [
            lax.dynamic_index_in_dim(ids, core_at, axis=0, keepdims=False),
            lax.dynamic_index_in_dim(ids_other, core_at, axis=0, keepdims=False),
        ]
    )
    shard = wanted // rows_dev
    inside = wanted - shard * rows_dev
    plane = inside // share
    line = inside - plane * share
    in_second = line >= pairs
    line_pair = jnp.where(in_second, line - pairs, line)
    step = (shard - depth_at) % depth
    flat = jnp.where(
        step == 0,
        plane * pairs + line_pair,
        4 * pairs + ((plane ^ plane_at) * (depth - 1) + step - 1) * pairs + line_pair,
    )
    diagonal = jnp.concatenate([tops[3], tops[4][:, : pairs - 128]], axis=1)
    lookup = jnp.concatenate(
        [own_pairs.reshape(-1, 384)]
        + [piece[:, :pairs].reshape(-1, 384) for piece in (tops[0], tops[1], tops[2], diagonal)],
        axis=0,
    )
    picked = lookup.at[flat.reshape(-1)].get(mode="promise_in_bounds").reshape(2, tokens, 384)
    picked = jnp.where(in_second[..., None], picked[..., 192:], picked[..., :192])
    rows_own = picked[0]
    rows_other = by_core(picked[1])

    ids_x = by_x(wanted)
    near = jnp.stack([wanted, ids_x])
    plane_ids = jnp.concatenate([near, by_y(near)], axis=0)
    t_shard = plane_ids // rows_dev
    t_inside = plane_ids - t_shard * rows_dev
    t_plane = t_inside // share
    target = jnp.where(
        t_plane == plane_at, ((t_shard - depth_at) % depth) * share + t_inside - t_plane * share, -1
    ).reshape(8, 1, tokens)

    cosine, sine, same = rotary_lanes(segments)
    position = jnp.arange(seq, dtype=jnp.int32)
    usable = same & (position[None, :, None] <= position[None, None, :]) & (live_mask[:, :, None] == 1)
    usable = usable | (position[None, :, None] == position[None, None, :])
    bias = jnp.where(usable, 0.0, masked_score).astype(F32)

    block = lambda w: pl.BlockSpec((seq, w), lambda i, *_: (i, 0))
    top_specs = [full(piece.shape) for piece in tops]
    low_specs = [full(piece.shape) for piece in lows]
    residual, queries, keys, values, qkv_full, out_full, up_full = kernel_call(
        project_kernel,
        coords,
        [rows_own, rows_other, embedded, up_proj, gain_one, w_qkv, w_out]
        + [p[:, :256] if i < 3 else p for i, p in enumerate(tops)]
        + [t if i in (3,) else t for i, t in enumerate(tops_other)]
        + list(lows) + list(lows_other) + [cosine, sine],
        [block(192), block(192), block(width), full(up_proj.shape), full((1, width)), full(w_qkv.shape), full(w_out.shape)]
        + [full((depth - 1, 256, 384)) if i < 3 else s for i, s in enumerate(top_specs)]
        + [full(t.shape) for t in tops_other] + low_specs + low_specs + [block(128), block(128)],
        [sds((tokens, width), F32)] + [sds((tokens, width), BF16)] * 3
        + [sds((2, width, 1152), BF16), sds((width, width), BF16), sds((384, width), BF16)],
        [block(width)] * 4 + [full((2, width, 1152)), full((width, width)), full((384, width))],
        (micro,),
        flops=2 * tokens * width * 2688,
        vmem=56,
        name="project",
    )

    pair_block = pl.BlockSpec((seq, 128), lambda s, p, *_: (s, p))
    seq_block = pl.BlockSpec((seq, width), lambda s, p, *_: (s, 0))
    attended, weights, middle, act_two = kernel_call(
        attend_kernel,
        coords,
        [queries, keys, values, bias, residual, out_full, gain_two],
        [pair_block, pair_block, pair_block, pl.BlockSpec((1, seq, seq), lambda s, p, *_: (s, 0, 0)), seq_block,
         pl.BlockSpec((128, width), lambda s, p, *_: (p, 0)), full((1, width))],
        [sds((tokens, width), BF16), sds((micro, 6, 2, seq, seq), BF16), sds((tokens, width), F32), sds((tokens, width), BF16)],
        [pair_block, pl.BlockSpec((1, 1, 2, seq, seq), lambda s, p, *_: (s, p, 0, 0, 0)), seq_block, seq_block],
        (micro, 6),
        scratch=[pltpu.VMEM((seq, width), F32)],
        flops=4 * tokens * seq * width + 2 * tokens * width * width,
        name="attend",
    )

    whole = full((tokens, width))
    output, ff_grads, grad_mid, grad_low, gain_two_grad = kernel_call(
        forward_kernel,
        coords,
        [act_two, cotangent, middle, gain_two, ff_gate_up, ff_gate_up, ff_down],
        [whole, whole, whole, full((1, width)),
         pl.BlockSpec((width, 512), lambda i, *_: (0, i)), pl.BlockSpec((width, 512), lambda i, *_: (0, i + 4)),
         pl.BlockSpec((512, width), lambda i, *_: (i, 0))],
        [sds((tokens, width), BF16), sds((8, 4, 288, 512), BF16), sds((tokens, width), F32), sds((tokens, width), BF16), sds((1, width), F32)],
        [whole, full((8, 4, 288, 512)), whole, whole, full((1, width))],
        (4,),
        scratch=[pltpu.VMEM((tokens, width), F32), pltpu.VMEM((tokens, width), F32), pltpu.VMEM((width, tokens), BF16)],
        flops=18 * tokens * width * 2048,
        vmem=60,
        name="feed",
    )
    ff_part = lax.psum_scatter(ff_grads, "oct", scatter_dimension=0, tiled=True)[0]

    back_block = pl.BlockSpec((tokens, 128), lambda p, *_: (0, p))
    (grad_projected,) = kernel_call(
        attend_back_kernel,
        coords,
        [queries, keys, values, weights, grad_low, out_full, cosine, sine],
        [back_block, back_block, back_block, pl.BlockSpec((micro, 1, 2, seq, seq), lambda p, *_: (0, p, 0, 0, 0)),
         whole, pl.BlockSpec((128, width), lambda p, *_: (p, 0)), full((tokens, 128)), full((tokens, 128))],
        [sds((3, tokens, width), BF16)],
        [pl.BlockSpec((3, tokens, 128), lambda p, *_: (0, 0, p))],
        (6,),
        flops=8 * tokens * seq * width + 2 * tokens * width * width,
        name="attend_back",
    )

    embedding_grad, grad_rows, act_one, gain_one_grad = kernel_call(
        embed_back_kernel,
        coords,
        [grad_projected, qkv_full, up_full, residual, grad_mid, gain_one],
        [pl.BlockSpec((3, seq, width), lambda i, *_: (0, i, 0)), full((2, width, 1152)), full((384, width)),
         block(width), block(width), full((1, width))],
        [sds((tokens, width), BF16), sds((2, seq, 384), BF16), sds((tokens, width), BF16), sds((1, width), F32)],
        [block(width), full((2, seq, 384)), block(width), full((1, width))],
        (micro,),
        flops=2 * tokens * width * 2688,
        name="embed_back",
    )

    mine = lax.dynamic_index_in_dim(grad_rows, core_at, axis=0, keepdims=False)
    other = by_core(lax.dynamic_index_in_dim(grad_rows, 1 - core_at, axis=0, keepdims=False))
    held = jnp.stack([mine, other])
    held_x, held_y = by_x(held), by_y(held)
    held_low, held_high = by_y(held_x[0]), by_x(held_y[1])

    gain_grads = jnp.concatenate([gain_one_grad, gain_two_grad], axis=0)
    (grads,) = kernel_call(
        weight_grad_kernel,
        coords,
        [act_one, grad_projected, attended, grad_low, rows_own, rows_other, embedding_grad, gain_grads],
        [whole, pl.BlockSpec((1, tokens, 384), lambda i, *_: (jnp.minimum(i, 5) // 2, 0, jnp.minimum(i, 5) % 2)), whole, whole,
         full((tokens, 192)), full((tokens, 192)), whole, full((2, width))],
        [sds((2, 4, 4, 64, 1536), BF16)],
        [full((2, 4, 4, 64, 1536))],
        (9,),
        scratch=[pltpu.VMEM((width, tokens), BF16), pltpu.VMEM((width, tokens), BF16)],
        flops=2 * tokens * width * 3456,
        name="weight_grad",
    )
    (table_sums,) = kernel_call(
        table_kernel,
        coords,
        [target, held, held_x, held_y, held_low, held_high],
        [pl.BlockSpec((1, 1, tokens), lambda i, *_: (i, 0, 0))] + [full((2, seq, 384))] * 3 + [full((seq, 384))] * 2,
        [sds((4, pairs, 384), BF16)],
        [full((4, pairs, 384))],
        (8,),
        scratch=[pltpu.VMEM((4 * share, 192), F32)],
        flops=2 * 8 * tokens * 4 * share * 192,
        name="table_sum",
    )

    weights_sum = reduce_all(grads, depth)
    table_sum = over_depth([table_sums[i] for i in range(depth)], depth)
    ff_sum = over_depth([ff_part[i] for i in range(depth)], depth)
    weights_sum, table_sum, ff_sum = (over_groups(v, groups).astype(BF16) for v in (weights_sum, table_sum, ff_sum))

    table_all = spread(table_sum, octet)
    weights_all = spread(weights_sum, octet)
    ff_all = lax.all_gather(ff_sum, "oct", axis=0)

    table_all = table_all.reshape(2, 4, pairs, 2, 192).transpose(0, 1, 3, 2, 4)
    table_grad = table_all.reshape(2, rows_dev, 192).astype(F32)
    tail = weights_all.reshape(2, 4, 64, 1536).astype(F32)
    qkv_grad = tail[:, :, 0:48, 0:1152].transpose(1, 2, 0, 3).reshape(192, 2304)
    out_grad = tail[:, :, 0:48, 1152:1536].transpose(1, 2, 0, 3).reshape(192, 768)
    up_all = jnp.concatenate([tail[:, :, 48:64, 0:384], tail[:, :, 48:64, 384:768]], axis=2)
    up_grad = up_all[:, :, 0:24].transpose(1, 2, 0, 3).reshape(96, 768)
    gains_grad = up_all[0, 0, 24].reshape(2, 192)
    ff_all = ff_all.astype(F32)
    gate_up_grad = ff_all[:, 0:192].transpose(1, 0, 2).reshape(192, 4096)
    down_right = jnp.concatenate([ff_all[:, 256:288, 0:256], ff_all[:, 256:288, 256:512]], axis=1)
    down_grad = jnp.concatenate([ff_all[:, 192:256], down_right], axis=2).reshape(512, 768)
    return (
        output.reshape(micro, 1, seq, width),
        embedding_grad.reshape(micro, 1, seq, width),
        table_grad,
        qkv_grad,
        out_grad,
        gate_up_grad,
        down_grad,
        up_grad,
        gains_grad,
    )


def solution(mesh):
    depth, rep = mesh.devices.shape
    groups = rep // 8
    fine = Mesh(mesh.devices.reshape(depth, groups, 8), ("fsdp", "grp", "oct"))
    every = ("fsdp", "grp", "oct")
    in_specs = (
        P(None, every, None, None),
        P(None, every, None, None),
        P(None, None, every, None),
        P(None, every, None),
        P(None, every, None),
        P(None, "fsdp", None),
        P("fsdp", None),
        P("fsdp", None),
        P("fsdp", None),
        P("fsdp", None),
        P("fsdp", None),
        P(None, "fsdp"),
    )
    out_specs = (
        P(None, every, None, None),
        P(None, every, None, None),
        P(None, "fsdp", None),
        P("fsdp", None),
        P("fsdp", None),
        P("fsdp", None),
        P("fsdp", None),
        P("fsdp", None),
        P(None, "fsdp"),
    )

    def step(*args):
        return body((depth, groups), *args)

    return jax.shard_map(step, mesh=fine, in_specs=in_specs, out_specs=out_specs, check_vma=False)
```

```python
import jax
import jax.numpy as jnp
import numpy as np
from jax import lax
from jax.experimental import pallas as pl
from jax.experimental.pallas import tpu as pltpu
from jax.sharding import Mesh, PartitionSpec as P

BF16 = jnp.bfloat16
F32 = jnp.float32
HEADS = 12
HEAD_DIM = 64
norm_eps = 1e-05
theta_base = 10000.0
masked_score = -1e30
MIB = 1 << 20

NN = (((1,), (0,)), ((), ()))
NT = (((1,), (1,)), ((), ()))
TN = (((0,), (0,)), ((), ()))


def mm(left, right, dims=NN):
    return lax.dot_general(left, right, dims, preferred_element_type=F32)


def sds(shape, dtype):
    return jax.ShapeDtypeStruct(shape, dtype)


def full(shape):
    return pl.BlockSpec(shape, lambda *_: (0,) * len(shape))


def kernel_call(
    kernel, coords, args, in_specs, out_shape, out_specs, grid, scratch=(), micros=5, vmem=60, name=None, after=(), aliases=()
):
    held = len(after)
    extra = [pl.BlockSpec(memory_space=pl.ANY)] * held

    def run(coords, *refs):
        kernel(coords, *refs[held:])

    return pl.pallas_call(
        run,
        out_shape=out_shape,
        grid_spec=pltpu.PrefetchScalarGridSpec(
            num_scalar_prefetch=1,
            grid=grid,
            in_specs=extra + list(in_specs),
            out_specs=out_specs,
            scratch_shapes=list(scratch),
        ),
        compiler_params=pltpu.CompilerParams(vmem_limit_bytes=vmem * MIB),
        input_output_aliases={1 + held + source: out for source, out in aliases},
        cost_estimate=pl.CostEstimate(flops=int(micros * 1.15e9), bytes_accessed=0, transcendentals=0),
        name=name,
    )(coords, *after, *args)


def by_core(value):
    return lax.ppermute(value, "oct", [(i, i ^ 1) for i in range(8)])


def by_x(value):
    return lax.ppermute(value, "oct", [(i, i ^ 2) for i in range(8)])


def by_y(value):
    return lax.ppermute(value, "oct", [(i, i ^ 4) for i in range(8)])


def from_ahead(value, step, size):
    return lax.ppermute(value, "fsdp", [((i + step) % size, i) for i in range(size)])


def to_ahead(value, step, size):
    return lax.ppermute(value, "fsdp", [(i, (i + step) % size) for i in range(size)])


def stack_kernel(coords, *refs):
    for at, ref in enumerate(refs[:-1]):
        refs[-1][at] = ref[...]


def cut_kernel(cut, coords, from_x, from_y, low, high):
    low[...] = from_x[:, :, 0:cut]
    high[...] = from_y[:, :, cut:]


def stack(coords, parts, after=()):
    shape = (len(parts),) + parts[0].shape
    return kernel_call(
        stack_kernel, coords, parts, [full(p.shape) for p in parts], [sds(shape, BF16)], [full(shape)], (1,),
        micros=1.5, vmem=16, name="stack", after=after,
    )[0]


def cut_pieces(coords, from_x, from_y, cut, after=()):
    shapes = [from_x.shape[:2] + (cut,), from_x.shape[:2] + (from_x.shape[2] - cut,)]
    return kernel_call(
        lambda *refs: cut_kernel(cut, *refs), coords, [from_x, from_y], [full(from_x.shape)] * 2,
        [sds(shape, BF16) for shape in shapes], [full(shape) for shape in shapes], (1,),
        micros=1.5, vmem=16, name="cut", after=after,
    )


def along_depth(piece, depth):
    return [from_ahead(piece, step, depth) for step in range(1, depth)]


def over_groups(value, groups):
    if groups > 1:
        value = lax.psum(value.astype(F32), "grp").astype(BF16)
    return value


def spread(value):
    from_x = by_x(value)
    four = [value, from_x, by_y(value), by_y(from_x)]
    return four + [by_core(piece) for piece in four]


def swap_halves(values):
    lane = lax.broadcasted_iota(jnp.int32, values.shape, 1)
    return jnp.where((lane & 63) < 32, pltpu.roll(values, 96, 1), pltpu.roll(values, 32, 1))


def prepare_table_kernel(coords, table, top):
    top[...] = table[0]


def prepare_low_kernel(coords, qkv, out, up, gains, low):
    low[:, 0:1152] = qkv[...]
    low[:, 1152:1536] = out[...]
    for g in range(2):
        for t in range(3):
            lane = 1536 + 128 * g
            low[16 * t : 16 * t + 16, lane : lane + 128] = up[16 * g : 16 * g + 16, 128 * t : 128 * t + 128]
    low[:, 1792:1920] = gains[...]


def prepare_feed_kernel(coords, gate_up, down_a, down_b, feed):
    for half, down in enumerate((down_a, down_b)):
        for shard in range(4):
            start = 512 * shard + 256 * half
            at = 1536 * half + 256 * shard
            feed[:, at : at + 256] = gate_up[:, start : start + 256]
        for g in range(4):
            for t in range(3):
                at = 1536 * half + 1024 + 128 * g
                feed[16 * t : 16 * t + 16, at : at + 128] = down[16 * g : 16 * g + 16, 128 * t : 128 * t + 128]


def assemble_kernel(
    coords, qkv_own, out_own, up_own, b0, bx, by, bl, bh, d0, dx, dy, dl, dh, w_pairs, w_out, w_up
):
    depth_at, plane_at, core_at = coords[0], coords[1], coords[2]
    w_up[pl.ds(pl.multiple_of(depth_at * 96, 32), 96), :] = up_own[...]
    base = pl.multiple_of(depth_at * 192, 64)
    for part in range(3):
        for p in range(6):
            at = 768 * part + 128 * p
            w_pairs[p, pl.ds(base, 192), 128 * part : 128 * part + 128] = qkv_own[:, at : at + 128]
    w_out[pl.ds(base, 192), :] = out_own[...]
    for core, lows in ((core_at, (b0, bx, by, bl, bh)), (1 - core_at, (d0, dx, dy, dl, dh))):
        column = pl.multiple_of(core * 384, 128)
        tiles = [core * 9 + t for t in range(9)]
        pairs_at = [t % 6 for t in tiles]
        lanes_at = [pl.multiple_of(t // 6 * 128, 128) for t in tiles]
        for far in range(4):
            plane = plane_at ^ far
            for step in range(1, 4):
                shard = (depth_at + step) % 4
                row = pl.multiple_of(shard * 192 + plane * 48, 16)
                if far < 3:
                    left, right = lows[far].at[step - 1, :, 0:1152], lows[far].at[step - 1, :, 1152:1920]
                else:
                    left, right = lows[3].at[step - 1], lows[4].at[step - 1]
                for t in range(9):
                    w_pairs[pairs_at[t], pl.ds(row, 48), pl.ds(lanes_at[t], 128)] = left[:, 128 * t : 128 * t + 128]
                w_out[pl.ds(row, 48), pl.ds(column, 384)] = right[:, 0:384]

                @pl.when(plane < 3)
                def _():
                    for g in range(2):
                        up_row = pl.multiple_of(shard * 96 + plane * 32 + 16 * g, 16)
                        for t in range(3):
                            lane = 384 + 128 * g
                            to = pl.ds(pl.multiple_of(core * 384 + 128 * t, 128), 128)
                            w_up[pl.ds(up_row, 16), to] = right[16 * t : 16 * t + 16, lane : lane + 128]


def lookup_kernel(coords, ids, table_own, t0, tx, ty, tl, th, rows_own, rows_other, table, total):
    plane_at = coords[1]
    at = pl.program_id(0)

    @pl.when(at == 0)
    def _():
        table[...] = table_own[0]
        total[...] = jnp.zeros_like(total)

    for step in range(1, 4):
        @pl.when(at == step)
        def _():
            for far, ref in enumerate((t0, tx, ty)):
                table[pl.ds(pl.multiple_of((plane_at ^ far) * 48, 16), 48), :] = ref[step - 1]
            last = pl.ds(pl.multiple_of((plane_at ^ 3) * 48, 16), 48)
            table[last, 0:896] = tl[step - 1]
            table[last, 896:1792] = th[step - 1]

    wanted = ids[...] - at * 1792
    line = lax.broadcasted_iota(jnp.int32, (256, 1536), 0)
    part = jnp.zeros((192, 1536), F32)
    for chunk in range(7):
        hot = jnp.where(line + 256 * chunk == wanted, 1.0, 0.0).astype(BF16)
        part += mm(table[:, 256 * chunk : 256 * chunk + 256], hot)
    total[...] += part

    @pl.when(at == 3)
    def _():
        rows_own[...] = total[:, 0:768].astype(BF16)
        rows_other[...] = total[:, 768:1536].astype(BF16)


def project_kernel(
    coords, rows_own, rows_other, embedded, w_up, gain, w_pair, cosine, sine,
    residual, act_out, queries, keys, values, act,
):
    core_at = coords[2]

    @pl.when(pl.program_id(0) == 0)
    def _():
        first = pl.multiple_of(core_at * 192, 64)
        second = pl.multiple_of(192 - core_at * 192, 64)
        x = embedded[...].astype(F32)
        x += mm(rows_own[...], w_up[pl.ds(first, 192), :], TN)
        x += mm(rows_other[...], w_up[pl.ds(second, 192), :], TN)
        residual[...] = x
        inverse = lax.rsqrt(jnp.mean(x * x, axis=-1, keepdims=True) + norm_eps)
        low = (x * inverse * gain[...]).astype(BF16)
        act[...] = low
        act_out[...] = low

    projected = mm(act[...], w_pair[0])
    cos, sin = cosine[...], sine[...]
    q, k = projected[:, 0:128], projected[:, 128:256]
    queries[0] = ((q * cos + swap_halves(q) * sin) * 0.125).astype(BF16)
    keys[0] = (k * cos + swap_halves(k) * sin).astype(BF16)
    values[0] = projected[:, 256:384].astype(BF16)


def attend_kernel(last, coords, queries, keys, values, bias, residual, w_out, *rest):
    if last:
        gain, weights_out, attended, middle, act_two, total = rest
    else:
        weights_out, attended, total = rest
    pair = pl.program_id(0)
    lane = lax.broadcasted_iota(jnp.int32, (384, 128), 1)
    columns = []
    for seq in range(2):
        rows = slice(384 * seq, 384 * seq + 384)
        q, k = queries[0, rows, :], keys[0, rows, :]
        v = values[0, rows, :]
        heads = []
        for head in range(2):
            q_head = jnp.where((lane >= 64) == (head == 1), q, jnp.zeros_like(q))
            scores = mm(k, q_head, NT) + bias[seq]
            top = jnp.max(scores, axis=0, keepdims=True)
            raised = jnp.exp(scores - top)
            weight = (raised * (1.0 / jnp.sum(raised, axis=0, keepdims=True))).astype(BF16)
            weights_out[0, seq, head] = weight
            heads.append(mm(weight, jnp.where((lane >= 64) == (head == 1), v, jnp.zeros_like(v)), TN))
        columns.append(heads[0] + heads[1])
    low = jnp.concatenate(columns, axis=0).astype(BF16)
    attended[0] = low
    part = mm(low, w_out[...])

    @pl.when(pair == 0)
    def _():
        total[...] = residual[...] + part

    @pl.when(pair > 0)
    def _():
        total[...] += part

    if not last:
        return

    @pl.when(pair == 2)
    def _():
        mid = total[...]
        middle[...] = mid
        inverse = lax.rsqrt(jnp.mean(mid * mid, axis=-1, keepdims=True) + norm_eps)
        act_two[...] = (mid * inverse * gain[...]).astype(BF16)


def feed_kernel(half, coords, act, cotangent, gate_up_own, down_own, b0, bx, by, bd, d0, dx, dy, dd, *rest):
    if half == 0:
        total, grad_act, grads, w_gate_up, w_down = rest
    else:
        (total_in, grad_act_in, middle, gain, attended_a, attended_b,
         output, grads, grad_mid, grad_low, gain_grad, total, grad_act, w_gate_up, w_down) = rest
    depth_at, plane_at, core_at = coords[0], coords[1], coords[2]
    at = pl.program_id(0)

    def assemble():
        base = pl.multiple_of(depth_at * 192, 64)
        for part in range(2):
            for shard in range(4):
                start = 2048 * part + 512 * shard + 256 * half
                w_gate_up[part, pl.ds(base, 192), 256 * shard : 256 * shard + 256] = gate_up_own[:, start : start + 256]
        w_down[pl.ds(pl.multiple_of(depth_at * 256, 256), 256), :] = down_own[256 * half : 256 * half + 256, :]
        for core, lows in ((core_at, (b0, bx, by, bd)), (1 - core_at, (d0, dx, dy, dd))):
            for far in range(4):
                plane = plane_at ^ far
                for step in range(1, 4):
                    shard = (depth_at + step) % 4
                    row = pl.multiple_of(shard * 192 + plane * 48, 16)
                    piece = lows[far].at[step - 1]
                    w_gate_up[core, pl.ds(row, 48), :] = piece[:, 0:1024]
                    for g in range(4):
                        for t in range(3):
                            row = pl.multiple_of(shard * 256 + plane * 64 + 16 * g, 16)
                            column = pl.multiple_of(core * 384 + 128 * t, 128)
                            lane = 1024 + 128 * g
                            w_down[pl.ds(row, 16), pl.ds(column, 128)] = piece[16 * t : 16 * t + 16, lane : lane + 128]

    @pl.when(at == 0)
    def _():
        total[...] = total_in[...] if half else jnp.zeros_like(total)
        grad_act[...] = grad_act_in[...] if half else jnp.zeros_like(grad_act)
        assemble()

    second = at
    units = pl.ds(pl.multiple_of(second * 512, 512), 512)
    a, c = act[...], cotangent[...]
    w_g, w_u, w_d = w_gate_up[0, :, units], w_gate_up[1, :, units], w_down[units, :]
    gate = mm(a, w_g)
    up = mm(a, w_u)
    back = mm(c, w_d, NT)
    sig = 0.5 * jnp.tanh(0.5 * gate) + 0.5
    silu = gate * sig
    inner = (silu * up).astype(BF16)
    d_up = (back * silu).astype(BF16)
    d_gate = (back * up * (sig * (1.0 + gate * (1.0 - sig)))).astype(BF16)
    total[...] += mm(inner, w_d)
    grad_act[...] += mm(d_gate, w_g, NT) + mm(d_up, w_u, NT)
    gate_g = mm(a, d_gate, TN).astype(BF16)
    up_g = mm(a, d_up, TN).astype(BF16)
    down = mm(inner, c, TN).astype(BF16)
    lanes = pl.ds(pl.multiple_of(second * 512, 512), 512)
    for plane in range(4):
        for core in range(2):
            q = 2 * plane + core
            block = up_g if core else gate_g
            for shard in range(4):
                row = 192 * shard + 48 * plane
                grads[q, (shard + 4 - depth_at) % 4, :, lanes] = block[row : row + 48, :]
            for b in range(2):
                for g in range(4):
                    low_lanes = slice(1024 + 128 * g, 1152 + 128 * g)
                    for t in range(3):
                        row = 256 * b + 64 * plane + 16 * g
                        column = 384 * core + 128 * t
                        grads[q, (2 * second + b + 4 - depth_at) % 4, 16 * t : 16 * t + 16, low_lanes] = down[
                            row : row + 16, column : column + 128
                        ]

    if half == 0:
        return

    @pl.when(at == 1)
    def _():
        mid = middle[...]
        output[...] = (mid + total[...]).astype(BF16)
        inverse = lax.rsqrt(jnp.mean(mid * mid, axis=-1, keepdims=True) + norm_eps)
        normed = mid * inverse
        grad = grad_act[...]
        gain_grad[...] = jnp.sum(grad * normed, axis=0, keepdims=True)
        n = grad * gain[...]
        g = cotangent[...].astype(F32) + inverse * (n - normed * jnp.mean(n * normed, axis=-1, keepdims=True))
        grad_mid[...] = g
        low = g.astype(BF16)
        grad_low[...] = low
        out_g = [mm(attended[p], low, TN) for attended in (attended_a, attended_b) for p in range(3)]
        out_g = jnp.concatenate(out_g, axis=0).astype(BF16)
        for plane in range(4):
            for core in range(2):
                for shard in range(4):
                    row = 192 * shard + 48 * plane
                    grads[2 * plane + core, (shard + 4 - depth_at) % 4, :, 1536:1920] = out_g[row : row + 48, 384 * core : 384 * core + 384]


def second_half_kernel(
    coords, queries, keys, values, weights_a, weights_b, grad_low, w_out, w_pair, cosine, sine,
    w_up, residual, grad_mid, gain,
    embedding_grad, grad_projected, rows_kept, rows_sent, gain_grad, grad_act,
):
    depth_at, plane_at, core_at = coords[0], coords[1], coords[2]
    step = pl.program_id(0)
    lane = lax.broadcasted_iota(jnp.int32, (384, 128), 1)

    @pl.when(step == 0)
    def _():
        grad_act[...] = jnp.zeros_like(grad_act)

    grad_attended = mm(grad_low[...], w_out[...], NT).astype(BF16)
    threes = []
    for seq in range(2):
        rows = slice(384 * seq, 384 * seq + 384)
        q, k, v, ga = queries[0, rows, :], keys[0, rows, :], values[0, rows, :], grad_attended[rows, :]
        grad_q = jnp.zeros((384, 128), F32)
        grad_k = jnp.zeros((384, 128), F32)
        grad_v = jnp.zeros((384, 128), F32)
        for head in range(2):
            mine = (lane >= 64) == (head == 1)
            ga_head = jnp.where(mine, ga, jnp.zeros_like(ga))
            q_head = jnp.where(mine, q, jnp.zeros_like(q))
            weight_low = jnp.where(step < 3, weights_a[0, seq, head], weights_b[0, seq, head])
            weight = weight_low.astype(F32)
            grad_weight = mm(v, ga_head, NT)
            row = jnp.sum(grad_weight * weight, axis=0, keepdims=True)
            grad_scores = (weight * (grad_weight - row)).astype(BF16)
            grad_v += mm(weight_low, ga_head)
            grad_k += mm(grad_scores, q_head)
            grad_q += mm(grad_scores, jnp.where(mine, k, jnp.zeros_like(k)), TN)
        grad_q = grad_q * 0.125
        cos, sin = cosine[rows, :], sine[rows, :]
        grad_q = (grad_q * cos - swap_halves(grad_q) * sin).astype(BF16)
        grad_k = (grad_k * cos - swap_halves(grad_k) * sin).astype(BF16)
        threes.append(jnp.concatenate([grad_q, grad_k, grad_v.astype(BF16)], axis=1))
    three = jnp.concatenate(threes, axis=0)
    grad_act[...] += mm(three, w_pair[0], NT)
    grad_projected[0] = three

    @pl.when(step == 5)
    def _():
        grad = grad_act[...]
        x = residual[...]
        inverse = lax.rsqrt(jnp.mean(x * x, axis=-1, keepdims=True) + norm_eps)
        normed = x * inverse
        gain_grad[...] = jnp.sum(grad * normed, axis=0, keepdims=True)
        n = grad * gain[...]
        g = grad_mid[...] + inverse * (n - normed * jnp.mean(n * normed, axis=-1, keepdims=True))
        low = g.astype(BF16)
        embedding_grad[...] = low
        rows = mm(w_up[...], low, NT).astype(BF16)

        @pl.when(core_at == 0)
        def _():
            rows_kept[...] = rows[0:192]
            rows_sent[...] = rows[192:384]

        @pl.when(core_at == 1)
        def _():
            rows_kept[...] = rows[192:384]
            rows_sent[...] = rows[0:192]


def both_ways(core_at, kept, sent, place):
    @pl.when(core_at == 0)
    def _():
        place(0, kept)
        place(1, sent)

    @pl.when(core_at == 1)
    def _():
        place(1, kept)
        place(0, sent)


def weight_grad_kernel(coords, act, grad_projected, kept, sent):
    depth_at, plane_at, core_at = coords[0], coords[1], coords[2]
    step = pl.program_id(0)
    weight_g = mm(act[...], grad_projected[0], TN)

    def place(core, out):
        for part in range(3):
            lanes = pl.ds(pl.multiple_of(512 + 768 * part + step * 128, 128), 128)
            for plane in range(4):
                for shard in range(4):
                    row = 192 * shard + 96 * core + 24 * plane
                    out[(shard + 4 - depth_at) % 4, plane ^ plane_at, :, lanes] = weight_g[
                        row : row + 24, 128 * part : 128 * part + 128
                    ].astype(BF16)

    both_ways(core_at, kept, sent, place)


def up_grad_kernel(
    coords, kept_in, sent_in, rows_own, rows_other, embedding_grad, gain_one_grad, gain_two_grad, kept, sent
):
    depth_at, plane_at, core_at = coords[0], coords[1], coords[2]
    low = embedding_grad[...]
    mine, other = mm(rows_own[...], low), mm(rows_other[...], low)
    first = jnp.where(core_at == 0, mine, other)
    second = jnp.where(core_at == 0, other, mine)
    both = jnp.concatenate([first, second], axis=0)
    one, two = gain_one_grad[...], gain_two_grad[...]

    def place(core, out):
        for plane in range(4):
            for shard in range(4):
                row = 96 * shard + 24 * plane
                far, near = (shard + 4 - depth_at) % 4, plane ^ plane_at
                out[far, near, :, 0:384] = both[row : row + 24, 384 * core : 384 * core + 384].astype(BF16)
                lines = jnp.zeros((24, 128), F32)
                if core == 0 and plane == 0:
                    start = 192 * shard
                    line = jnp.concatenate([one[:, start : start + 192], two[:, start : start + 192]], axis=1)
                    lines = jnp.concatenate(
                        [line[:, 0:128], line[:, 128:256], line[:, 256:384], jnp.zeros((21, 128), F32)], axis=0
                    )
                out[far, near, :, 384:512] = lines.astype(BF16)

    both_ways(core_at, kept, sent, place)


def table_add(ids, ref, total):
    line = lax.broadcasted_iota(jnp.int32, (2048, 768), 0)
    hot = jnp.where(line == ids[0], 1.0, 0.0).astype(BF16)
    total[...] += mm(ref[0] if len(ref.shape) == 3 else ref[...], hot, NT)


def table_kernel(sources, first, coords, ids, *rest):
    refs = rest[:sources]
    total = rest[-1]
    at = pl.program_id(0)

    @pl.when(at == 0)
    def _():
        total[...] = jnp.zeros_like(total) if first else rest[sources][...]

    for source, ref in enumerate(refs):
        @pl.when(at == source)
        def _():
            table_add(ids, ref, total)


def table_last_kernel(coords, ids, low, high, before, kept_x, kept_y, got_y, got_x, *rest):
    outs, total = rest[:4], rest[4]
    at = pl.program_id(0)

    @pl.when(at == 0)
    def _():
        total[...] = before[...]
        table_add(ids, low, total)
        for i in range(2):
            outs[i][:, 0:2816] = (kept_x[i].astype(F32) + got_y[i].astype(F32)).astype(BF16)
            outs[i + 2][:, 0:2816] = (kept_y[i].astype(F32) + got_x[i].astype(F32)).astype(BF16)

    @pl.when(at == 1)
    def _():
        table_add(ids, high, total)
        for shard in range(4):
            for g in range(8):
                lane = 2816 + 512 * g
                outs[shard][:, lane : lane + 512] = total[24 * g : 24 * g + 24, 512 * shard : 512 * shard + 512].astype(BF16)


def add_kernel(coords, *refs):
    total = refs[0][...].astype(F32)
    for ref in refs[1:-1]:
        total = total + ref[...].astype(F32)
    refs[-1][...] = total.astype(BF16)


def join_kernel(coords, first, *refs):
    refs[-1][:, 0:1536] = first[...]
    total = refs[0][...].astype(F32)
    for ref in refs[1:-1]:
        total = total + ref[...].astype(F32)
    refs[-1][:, 1536:3456] = total.astype(BF16)


def add_all(coords, parts, after=()):
    shape = parts[0].shape
    return kernel_call(
        add_kernel, coords, parts, [full(shape)] * len(parts), [sds(shape, BF16)], [full(shape)], (1,),
        micros=1.5, vmem=16, name="add", after=after,
    )[0]


def split_kernel(coords, value, *parts):
    for at, part in enumerate(parts):
        part[...] = value[0, at]


def first_sum_kernel(coords, kept, got, send_x, send_y, keep_x, keep_y):
    for shard in range(4):
        for plane in range(4):
            value = (kept[shard, plane].astype(F32) + got[shard, plane].astype(F32)).astype(BF16)
            if shard < 2:
                (send_x if plane % 2 else keep_x)[shard, plane // 2] = value
            else:
                (send_y if plane // 2 else keep_y)[shard - 2, plane % 2] = value


def second_sum_kernel(coords, keep_x, keep_y, got_x, got_y, send_y, send_x, kept_x, kept_y):
    for i in range(2):
        send_y[i] = (keep_x[i, 1].astype(F32) + got_x[i, 1].astype(F32)).astype(BF16)
        send_x[i] = (keep_y[i, 1].astype(F32) + got_y[i, 1].astype(F32)).astype(BF16)
        kept_x[i] = (keep_x[i, 0].astype(F32) + got_x[i, 0].astype(F32)).astype(BF16)
        kept_y[i] = (keep_y[i, 0].astype(F32) + got_y[i, 0].astype(F32)).astype(BF16)


def each_piece(coords, refs):
    for index, ref in enumerate(refs):
        yield coords[2] ^ (index // 4), coords[1] ^ (index % 4), ref


def finish_feed_kernel(coords, *refs):
    gate_up, down, out = refs[8:]
    for core, plane, ref in each_piece(coords, refs[0:8]):
        rows = pl.ds(pl.multiple_of(plane * 48, 16), 48)
        for half in range(2):
            for j in range(4):
                lanes = pl.ds(pl.multiple_of(core * 2048 + 512 * j + 256 * half, 256), 256)
                at = 1536 * half + 256 * j
                gate_up[rows, lanes] = ref[:, at : at + 256].astype(F32)
            for g in range(4):
                for t in range(3):
                    low_rows = pl.ds(pl.multiple_of(256 * half + plane * 64 + 16 * g, 16), 16)
                    lanes = pl.ds(pl.multiple_of(core * 384 + 128 * t, 128), 128)
                    at = 1536 * half + 1024 + 128 * g
                    down[low_rows, lanes] = ref[16 * t : 16 * t + 16, at : at + 128].astype(F32)
        out[rows, pl.ds(pl.multiple_of(core * 384, 128), 384)] = ref[:, 3072:3456].astype(F32)


def finish_rest_kernel(coords, *refs):
    qkv, up, gains, table = refs[8:]
    for core, plane, ref in each_piece(coords, refs[0:8]):
        rows = pl.ds(pl.multiple_of(core * 96 + plane * 24, 8), 24)
        qkv[rows, :] = ref[:, 512:2816].astype(F32)
        up_rows = pl.ds(pl.multiple_of(plane * 24, 8), 24)
        up[up_rows, pl.ds(pl.multiple_of(core * 384, 128), 384)] = ref[:, 0:384].astype(F32)
        for g in range(8):
            lane = 2816 + 512 * g
            at = pl.ds(pl.multiple_of(plane * 512, 512), 256)
            table[core, 24 * g : 24 * g + 24, at] = ref[:, lane : lane + 256].astype(F32)

        @pl.when(plane < 3)
        def _():
            for g in range(8):
                lane = 2816 + 512 * g + 256
                at = pl.ds(pl.multiple_of(plane * 512 + 256, 256), 256)
                table[core, 24 * g : 24 * g + 24, at] = ref[:, lane : lane + 256].astype(F32)

        @pl.when((core == 0) & (plane == 0))
        def _():
            value = ref[:, 384:512].astype(F32)
            line = jnp.concatenate([value[i : i + 1] for i in range(3)], axis=1)
            gains[0:1, :] = line[:, 0:192]
            gains[1:2, :] = line[:, 192:384]


def rotary_lanes(segments):
    seq_len = segments.shape[-1]
    position = jnp.arange(seq_len, dtype=jnp.int32)
    same = segments[:, :, None] == segments[:, None, :]
    start = jnp.min(jnp.where(same, position[None, None, :], seq_len), axis=-1)
    offset = (position[None, :] - start).astype(F32)
    half = HEAD_DIM // 2
    frequency = theta_base ** (-jnp.arange(half, dtype=F32) / half)
    angle = offset[..., None] * frequency
    cos, sin = jnp.cos(angle), jnp.sin(angle)
    cosine = jnp.concatenate([cos, cos, cos, cos], axis=-1)
    sine = jnp.concatenate([-sin, sin, -sin, sin], axis=-1)
    return cosine.reshape(-1, 128), sine.reshape(-1, 128), same


def body(
    sizes, embedded, cotangent, ngram_ids, segments, live_mask, tables, w_qkv, w_out, w_gate_up, w_down, up_proj, norm_gains
):
    depth, groups = sizes
    micro, _, seq, width = embedded.shape
    tokens = micro * seq
    rows_dev = tables.shape[1]
    depth_at = lax.axis_index("fsdp")
    octet = lax.axis_index("oct")
    core_at = octet & 1
    plane_at = octet >> 1
    coords = jnp.stack([depth_at, plane_at, core_at]).astype(jnp.int32)
    embedded = embedded.reshape(tokens, width)
    cotangent = cotangent.reshape(tokens, width)
    segments = segments.reshape(micro, seq)
    live_mask = live_mask.reshape(micro, seq)
    ids = ngram_ids.reshape(2, tokens)
    tables_t = jnp.transpose(tables, (0, 2, 1))

    gain_block = jnp.pad(norm_gains.reshape(3, 128), ((0, 45), (0, 0)))
    (top,) = kernel_call(
        prepare_table_kernel,
        coords,
        [tables_t],
        [pl.BlockSpec((1, 48, rows_dev), lambda i, at: (at[2], at[1], 0))],
        [sds((48, rows_dev), BF16)],
        [full((48, rows_dev))],
        (1,),
        micros=1,
        name="prepare_table",
    )
    top_held = stack(coords, along_depth(top, depth))
    top_x, top_y = by_x(top_held), by_y(top_held)
    (low,) = kernel_call(
        prepare_low_kernel,
        coords,
        [w_qkv, w_out, up_proj, gain_block],
        [
            pl.BlockSpec((48, 1152), lambda i, at: (at[1], at[2])),
            pl.BlockSpec((48, 384), lambda i, at: (at[1], at[2])),
            pl.BlockSpec((32, 384), lambda i, at: (jnp.minimum(at[1], 2), at[2])),
            full((48, 128)),
        ],
        [sds((48, 1920), BF16)],
        [full((48, 1920))],
        (1,),
        micros=1,
        name="prepare_low",
        after=[top_held],
    )
    low_steps = along_depth(low, depth)
    top_low, top_high = cut_pieces(coords, top_x, top_y, 896)
    low_held = stack(coords, low_steps, after=[top_low])
    low_x, low_y = by_x(low_held), by_y(low_held)
    tops = [top_held, top_x, top_y, by_y(top_low), by_x(top_high)]
    (feed,) = kernel_call(
        prepare_feed_kernel,
        coords,
        [w_gate_up, w_down, w_down],
        [
            pl.BlockSpec((48, 2048), lambda i, at: (at[1], at[2])),
            pl.BlockSpec((64, 384), lambda i, at: (at[1], at[2])),
            pl.BlockSpec((64, 384), lambda i, at: (4 + at[1], at[2])),
        ],
        [sds((48, 3072), BF16)],
        [full((48, 3072))],
        (1,),
        micros=1,
        name="prepare_feed",
        after=[low_held],
    )

    feed_steps = along_depth(feed, depth)

    gains_rel = jnp.concatenate([norm_gains[None], low_held[:, 0:3, 1792:1920].reshape(depth - 1, 2, 192)], axis=0)
    gains = jnp.roll(gains_rel, depth_at, axis=0).transpose(1, 0, 2).reshape(2, width).astype(F32)
    gain_one, gain_two = gains[0:1], gains[1:2]

    ids_other = by_core(ids)
    wanted = jnp.concatenate(
        [
            lax.dynamic_index_in_dim(ids, core_at, axis=0),
            lax.dynamic_index_in_dim(ids_other, core_at, axis=0),
        ],
        axis=0,
    )
    shard = wanted // rows_dev
    inside = wanted - shard * rows_dev
    line = ((shard - depth_at) % depth) * rows_dev + inside
    rows_own, rows_sent = kernel_call(
        lookup_kernel,
        coords,
        [line.reshape(1, 2 * tokens), tables_t] + list(tops),
        [full((1, 2 * tokens)), pl.BlockSpec((1, 192, rows_dev), lambda i, at: (at[2], 0, 0))] + [full(t.shape) for t in tops],
        [sds((192, tokens), BF16)] * 2,
        [full((192, tokens))] * 2,
        (4,),
        scratch=[pltpu.VMEM((192, rows_dev), BF16), pltpu.VMEM((192, 2 * tokens), F32)],
        micros=8,
        name="lookup",
        after=[low_held, feed],
    )
    rows_other = by_core(rows_sent)

    low_low, low_high = cut_pieces(coords, low_x, low_y, 1152, after=[rows_sent])
    lows = [low_held, low_x, low_y, by_y(low_low), by_x(low_high)]
    gathered = lows + [by_core(piece) for piece in lows]
    feed_held = stack(coords, feed_steps, after=[low_low])
    feed_x, feed_y = by_x(feed_held), by_y(feed_held)
    w_pairs, w_out_full, w_up_full = kernel_call(
        assemble_kernel,
        coords,
        [w_qkv, w_out, up_proj] + gathered,
        [full(a.shape) for a in [w_qkv, w_out, up_proj] + gathered],
        [sds((6, width, 384), BF16), sds((width, width), BF16), sds((384, width), BF16)],
        [full((6, width, 384)), full((width, width)), full((384, width))],
        (1,),
        vmem=32,
        name="assemble",
        after=[feed_held],
    )

    near = jnp.stack([wanted, by_x(wanted)])
    plane_ids = jnp.concatenate([near, by_y(near)], axis=0)
    t_shard = plane_ids // rows_dev
    t_inside = plane_ids - t_shard * rows_dev
    target = jnp.where(
        t_inside // 512 == plane_at, ((t_shard - depth_at) % depth) * 512 + t_inside % 512, -1
    ).reshape(8, 1, tokens)

    cosine, sine, same = rotary_lanes(segments)
    position = jnp.arange(seq, dtype=jnp.int32)
    usable = same & (position[None, :, None] <= position[None, None, :]) & (live_mask[:, :, None] == 1)
    usable = usable | (position[None, :, None] == position[None, None, :])
    bias = jnp.where(usable, 0.0, masked_score).astype(F32)

    whole = full((tokens, width))
    line_spec = full((1, width))
    turn = full((tokens, 128))

    def pair_block(start):
        return pl.BlockSpec((1, tokens, 128), lambda p, *_: (p + start, 0, 0))

    residual, act_one, queries, keys, values = kernel_call(
        project_kernel,
        coords,
        [rows_own, rows_other, embedded, w_up_full, gain_one, w_pairs, cosine, sine],
        [full((192, tokens))] * 2
        + [whole, full((384, width)), line_spec, pl.BlockSpec((1, width, 384), lambda p, *_: (p, 0, 0)), turn, turn],
        [sds((tokens, width), F32), sds((tokens, width), BF16)] + [sds((6, tokens, 128), BF16)] * 3,
        [whole, whole] + [pair_block(0)] * 3,
        (6,),
        scratch=[pltpu.VMEM((tokens, width), BF16)],
        micros=12,
        name="project",
        after=[target],
    )

    def attend_call(start, before, extra, extra_specs, outs, out_specs, after):
        return kernel_call(
            lambda *refs: attend_kernel(start > 0, *refs),
            coords,
            [queries, keys, values, bias, before, w_out_full] + extra,
            [pair_block(start)] * 3
            + [full((micro, seq, seq)), whole, pl.BlockSpec((128, width), lambda p, *_: (p + start, 0))] + extra_specs,
            [sds((3, micro, 2, seq, seq), BF16), sds((3, tokens, 128), BF16)] + outs,
            [pl.BlockSpec((1, micro, 2, seq, seq), lambda p, *_: (p, 0, 0, 0, 0)),
             pair_block(0)] + out_specs,
            (3,),
            scratch=[pltpu.VMEM((tokens, width), F32)] if start else [],
            micros=12,
            name="attend",
            after=after,
        )

    feed_low, feed_high = cut_pieces(coords, feed_x, feed_y, 1536, after=[queries])
    feed_low, feed_high = by_y(feed_low), by_x(feed_high)
    weights_a, attended_a, partial = attend_call(0, residual, [], [], [sds((tokens, width), F32)], [whole], [])
    weights_b, attended_b, middle, act_two = attend_call(
        3, partial, [gain_two], [line_spec],
        [sds((tokens, width), F32), sds((tokens, width), BF16)], [whole, whole],
        [feed_low, feed_high],
    )
    wholes = [feed_held, feed_x, feed_y]
    others = [by_core(piece) for piece in wholes]
    feed_parts = [wholes + [feed_low] + others + [by_core(feed_low)], wholes + [feed_high] + others + [by_core(feed_high)]]

    def single(shape):
        return pl.BlockSpec(shape, lambda *_: (0,) * len(shape), pipeline_mode=pl.Buffered(1))

    one = single((tokens, width))
    feed_scratch = [pltpu.VMEM((2, width, 1024), BF16), pltpu.VMEM((1024, width), BF16)]

    def feed_specs(half):
        part = pl.BlockSpec((depth - 1, 48, 1536), lambda *_: (0, 0, half), pipeline_mode=pl.Buffered(1))
        return [one, one, single(w_gate_up.shape), single(w_down.shape)] + ([part] * 3 + [single((depth - 1, 48, 1536))]) * 2

    feed_in = [act_two, cotangent, w_gate_up, w_down]
    grads_shapes = [(8, depth, 48, 1536), (8, depth, 48, 1920)]
    total, grad_act, feed_grads = kernel_call(
        lambda *refs: feed_kernel(0, *refs),
        coords,
        feed_in + feed_parts[0],
        feed_specs(0),
        [sds((tokens, width), F32), sds((tokens, width), F32), sds(grads_shapes[0], BF16)],
        [one, one, single(grads_shapes[0])],
        (2,),
        scratch=feed_scratch,
        micros=20,
        name="feed_first",
    )
    feed_part_a = lax.psum_scatter(feed_grads, "oct", scatter_dimension=0, tiled=True)
    output, feed_grads, grad_mid, grad_low, gain_two_grad = kernel_call(
        lambda *refs: feed_kernel(1, *refs),
        coords,
        feed_in + feed_parts[1] + [total, grad_act, middle, gain_two, attended_a, attended_b],
        feed_specs(1) + [one, one, one, line_spec] + [single((3, tokens, 128))] * 2,
        [sds((tokens, width), BF16), sds(grads_shapes[1], BF16), sds((tokens, width), F32), sds((tokens, width), BF16),
         sds((1, width), F32)],
        [one, single(grads_shapes[1]), one, one, line_spec],
        (2,),
        scratch=[pltpu.VMEM((tokens, width), F32)] * 2 + feed_scratch,
        micros=24,
        name="feed_second",
    )
    feed_part_b = lax.psum_scatter(feed_grads, "oct", scatter_dimension=0, tiled=True)

    def steps_block(shape, place):
        return pl.BlockSpec(shape, lambda p, *_: place(p) + (0,) * (len(shape) - 1))

    tail_shape = sds((4, 4, 24, 2816), BF16)
    weights_shape = (1, micro, 2, seq, seq)
    embedding_grad, grad_projected, rows_kept, rows_sent, gain_one_grad = kernel_call(
        second_half_kernel,
        coords,
        [queries, keys, values, weights_a, weights_b, grad_low, w_out_full, w_pairs, cosine, sine, w_up_full, residual,
         grad_mid, gain_one],
        [pair_block(0)] * 3
        + [steps_block(weights_shape, lambda p: (jnp.minimum(p, 2),)), steps_block(weights_shape, lambda p: (jnp.maximum(p - 3, 0),)),
           whole, pl.BlockSpec((128, width), lambda p, *_: (p, 0)), pl.BlockSpec((1, width, 384), lambda p, *_: (p, 0, 0)),
           turn, turn, full((384, width)), whole, whole, line_spec],
        [sds((tokens, width), BF16), sds((6, tokens, 384), BF16), sds((192, tokens), BF16), sds((192, tokens), BF16),
         sds((1, width), F32)],
        [whole, pl.BlockSpec((1, tokens, 384), lambda p, *_: (p, 0, 0)), full((192, tokens)), full((192, tokens)), line_spec],
        (6,),
        scratch=[pltpu.VMEM((tokens, width), F32)],
        micros=36,
        name="second_half",
    )

    rows_got = by_core(rows_sent)
    held = stack(coords, [rows_kept, rows_got])
    held_x, held_y = by_x(held), by_y(held)
    kept_c, sent_c = kernel_call(
        weight_grad_kernel,
        coords,
        [act_one, grad_projected],
        [whole, pl.BlockSpec((1, tokens, 384), lambda p, *_: (p, 0, 0))],
        [tail_shape, tail_shape],
        [full(tail_shape.shape)] * 2,
        (6,),
        micros=9,
        name="weight_grad",
        after=[held],
    )

    def split_call(part, after):
        shape = part.shape[2:]
        shards = kernel_call(
            split_kernel, coords, [part], [full(part.shape)], [sds(shape, BF16)] * depth, [full(shape)] * depth,
            (1,), micros=2, vmem=16, name="split", after=after,
        )
        return [shards[0]] + [to_ahead(shards[step], step, depth) for step in range(1, depth)]

    feed_got_a = split_call(feed_part_a, [kept_c])
    held_low, held_high = held_x[0], held_y[1]
    up_block = pl.BlockSpec((4, 4, 24, 512), lambda *_: (0, 0, 0, 0))
    kept_c, sent_c = kernel_call(
        up_grad_kernel,
        coords,
        [kept_c, sent_c, rows_own, rows_other, embedding_grad, gain_one_grad, gain_two_grad],
        [pl.BlockSpec(memory_space=pl.ANY)] * 2
        + [full((192, tokens)), full((192, tokens)), whole, line_spec, line_spec],
        [tail_shape, tail_shape],
        [up_block, up_block],
        (1,),
        micros=3,
        vmem=24,
        name="up_grad",
        after=[held_low, held_high],
        aliases=[(0, 0), (1, 1)],
    )
    held_low, held_high = by_y(held_low), by_x(held_high)
    got_c = by_core(sent_c)

    part_shape, low_shape = (2, 2, 24, 2816), (2, 24, 2816)
    send_x, send_y, keep_x, keep_y = kernel_call(
        first_sum_kernel, coords, [kept_c, got_c], [full(tail_shape.shape)] * 2, [sds(part_shape, BF16)] * 4,
        [full(part_shape)] * 4, (1,), micros=3, vmem=24, name="first_sum",
    )
    c_x, c_y = by_x(send_x), by_y(send_y)

    def table_call(sources, refs, places, before, after):
        specs = [pl.BlockSpec((1, 192, tokens), lambda i, *_, place=place: (place, 0, 0)) for place in places]
        return kernel_call(
            lambda *r: table_kernel(len(refs), before is None, *r),
            coords,
            [target[sources]] + refs + ([] if before is None else [before]),
            [pl.BlockSpec((1, 1, tokens), lambda i, *_: (i, 0, 0))] + specs + ([] if before is None else [full((192, 2048))]),
            [sds((192, 2048), F32)],
            [full((192, 2048))],
            (len(refs),),
            micros=3 + len(refs),
            vmem=24,
        name="table_sum",
            after=after,
        )[0]

    sums = table_call(slice(0, 2), [held, held], [0, 1], None, [send_x])
    feed_sum_a = add_all(coords, feed_got_a, [send_x])
    send_y, send_x, kept_x, kept_y = kernel_call(
        second_sum_kernel, coords, [keep_x, keep_y, c_x, c_y], [full(part_shape)] * 4, [sds(low_shape, BF16)] * 4,
        [full(low_shape)] * 4, (1,), micros=2, vmem=16, name="second_sum", after=[feed_sum_a],
    )
    c_y, c_x = by_y(send_y), by_x(send_x)
    feed_got_b = split_call(feed_part_b, [send_y])
    sums = table_call(slice(2, 6), [held_x, held_x, held_y, held_y], [0, 1, 0, 1], sums, [feed_got_b[0]])
    shard_shape = (24, 6912)
    shards = kernel_call(
        table_last_kernel,
        coords,
        [target[6:8], held_low, held_high, sums, kept_x, kept_y, c_y, c_x],
        [pl.BlockSpec((1, 1, tokens), lambda i, *_: (i, 0, 0))] + [full((192, tokens))] * 2 + [full((192, 2048))]
        + [full(low_shape)] * 4,
        [sds(shard_shape, BF16)] * 4,
        [full(shard_shape)] * 4,
        (2,),
        scratch=[pltpu.VMEM((192, 2048), F32)],
        micros=6,
        vmem=24,
        name="table_last",
    )
    tail_got = [shards[0]] + [to_ahead(shards[step], step, depth) for step in range(1, depth)]
    pieces = spread(over_groups(add_all(coords, tail_got), groups))
    feed_sum = kernel_call(
        join_kernel, coords, [feed_sum_a] + feed_got_b, [full((48, 1536))] + [full((48, 1920))] * 4, [sds((48, 3456), BF16)],
        [full((48, 3456))], (1,), micros=2, vmem=16, name="join", after=[shards[0]],
    )[0]
    feed_pieces = spread(over_groups(feed_sum, groups))

    def finish(kernel, refs, outs, name):
        return kernel_call(
            kernel, coords, refs, [full(r.shape) for r in refs], outs, [full(o.shape) for o in outs], (1,), vmem=32, name=name
        )

    gate_up_grad, down_grad, out_grad = finish(
        finish_feed_kernel,
        feed_pieces,
        [sds((192, 4096), F32), sds((512, width), F32), sds((192, width), F32)],
        "finish_feed",
    )
    qkv_grad, up_grad, gains_grad, table_grad = finish(
        finish_rest_kernel,
        pieces,
        [sds((192, 2304), F32), sds((96, width), F32), sds((2, 192), F32), sds((2, 192, rows_dev), F32)],
        "finish_rest",
    )
    return (
        output.reshape(micro, 1, seq, width),
        embedding_grad.reshape(micro, 1, seq, width),
        jnp.transpose(table_grad, (0, 2, 1)),
        qkv_grad,
        out_grad,
        gate_up_grad,
        down_grad,
        up_grad,
        gains_grad,
    )


def solution(mesh):
    depth, rep = mesh.devices.shape
    groups = rep // 8
    fine = Mesh(mesh.devices.reshape(depth, groups, 8), ("fsdp", "grp", "oct"))
    every = ("fsdp", "grp", "oct")
    in_specs = (
        P(None, every, None, None),
        P(None, every, None, None),
        P(None, None, every, None),
        P(None, every, None),
        P(None, every, None),
        P(None, "fsdp", None),
        P("fsdp", None),
        P("fsdp", None),
        P("fsdp", None),
        P("fsdp", None),
        P("fsdp", None),
        P(None, "fsdp"),
    )
    out_specs = (
        P(None, every, None, None),
        P(None, every, None, None),
        P(None, "fsdp", None),
        P("fsdp", None),
        P("fsdp", None),
        P("fsdp", None),
        P("fsdp", None),
        P("fsdp", None),
        P(None, "fsdp"),
    )

    def step(*args):
        return body((depth, groups), *args)

    return jax.shard_map(step, mesh=fine, in_specs=in_specs, out_specs=out_specs, check_vma=False)
```

```python
import jax
import jax.numpy as jnp
import numpy as np
from jax import lax
from jax.experimental import pallas as pl
from jax.experimental.pallas import tpu as pltpu
from jax.sharding import Mesh, PartitionSpec as P

BF16 = jnp.bfloat16
F32 = jnp.float32
HEADS = 12
HEAD_DIM = 64
norm_eps = 1e-05
theta_base = 10000.0
masked_score = -1e30
MIB = 1 << 20

NN = (((1,), (0,)), ((), ()))
NT = (((1,), (1,)), ((), ()))
TN = (((0,), (0,)), ((), ()))


def mm(left, right, dims=NN):
    return lax.dot_general(left, right, dims, preferred_element_type=F32)


def sds(shape, dtype):
    return jax.ShapeDtypeStruct(shape, dtype)


def full(shape):
    return pl.BlockSpec(shape, lambda *_: (0,) * len(shape))


def kernel_call(
    kernel, coords, args, in_specs, out_shape, out_specs, grid, scratch=(), micros=5, vmem=60, name=None, after=(), aliases=()
):
    held = len(after)
    extra = [pl.BlockSpec(memory_space=pl.ANY)] * held

    def run(coords, *refs):
        kernel(coords, *refs[held:])

    return pl.pallas_call(
        run,
        out_shape=out_shape,
        grid_spec=pltpu.PrefetchScalarGridSpec(
            num_scalar_prefetch=1,
            grid=grid,
            in_specs=extra + list(in_specs),
            out_specs=out_specs,
            scratch_shapes=list(scratch),
        ),
        compiler_params=pltpu.CompilerParams(vmem_limit_bytes=vmem * MIB),
        input_output_aliases={1 + held + source: out for source, out in aliases},
        cost_estimate=pl.CostEstimate(flops=int(micros * 1.15e9), bytes_accessed=0, transcendentals=0),
        name=name,
    )(coords, *after, *args)


def by_core(value):
    return lax.ppermute(value, "oct", [(i, i ^ 1) for i in range(8)])


def by_x(value):
    return lax.ppermute(value, "oct", [(i, i ^ 2) for i in range(8)])


def by_y(value):
    return lax.ppermute(value, "oct", [(i, i ^ 4) for i in range(8)])


def from_ahead(value, step, size):
    return lax.ppermute(value, "fsdp", [((i + step) % size, i) for i in range(size)])


def to_ahead(value, step, size):
    return lax.ppermute(value, "fsdp", [(i, (i + step) % size) for i in range(size)])


def stack_kernel(coords, *refs):
    for at, ref in enumerate(refs[:-1]):
        refs[-1][at] = ref[...]


def cut_kernel(cut, coords, from_x, from_y, low, high):
    low[...] = from_x[:, :, 0:cut]
    high[...] = from_y[:, :, cut:]


def stack(coords, parts, after=()):
    shape = (len(parts),) + parts[0].shape
    return kernel_call(
        stack_kernel, coords, parts, [full(p.shape) for p in parts], [sds(shape, BF16)], [full(shape)], (1,),
        micros=1.5, vmem=16, name="stack", after=after,
    )[0]


def cut_pieces(coords, from_x, from_y, cut, after=()):
    shapes = [from_x.shape[:2] + (cut,), from_x.shape[:2] + (from_x.shape[2] - cut,)]
    return kernel_call(
        lambda *refs: cut_kernel(cut, *refs), coords, [from_x, from_y], [full(from_x.shape)] * 2,
        [sds(shape, BF16) for shape in shapes], [full(shape) for shape in shapes], (1,),
        micros=1.5, vmem=16, name="cut", after=after,
    )


def along_depth(piece, depth):
    return [from_ahead(piece, step, depth) for step in range(1, depth)]


def over_groups(value, groups):
    if groups > 1:
        value = lax.psum(value.astype(F32), "grp").astype(BF16)
    return value


def spread(value):
    from_x = by_x(value)
    four = [value, from_x, by_y(value), by_y(from_x)]
    return four + [by_core(piece) for piece in four]


def swap_halves(values):
    lane = lax.broadcasted_iota(jnp.int32, values.shape, 1)
    return jnp.where((lane & 63) < 32, pltpu.roll(values, 96, 1), pltpu.roll(values, 32, 1))


def prepare_table_kernel(coords, table, top):
    top[...] = table[0]


def prepare_low_kernel(coords, qkv, out, up, gains, low):
    low[:, 0:1152] = qkv[...]
    low[:, 1152:1536] = out[...]
    for g in range(2):
        for t in range(3):
            lane = 1536 + 128 * g
            low[16 * t : 16 * t + 16, lane : lane + 128] = up[16 * g : 16 * g + 16, 128 * t : 128 * t + 128]
    low[:, 1792:1920] = gains[...]


def prepare_feed_kernel(coords, gate_up, down_a, down_b, feed):
    for half, down in enumerate((down_a, down_b)):
        for shard in range(4):
            start = 512 * shard + 256 * half
            at = 1536 * half + 256 * shard
            feed[:, at : at + 256] = gate_up[:, start : start + 256]
        for g in range(4):
            for t in range(3):
                at = 1536 * half + 1024 + 128 * g
                feed[16 * t : 16 * t + 16, at : at + 128] = down[16 * g : 16 * g + 16, 128 * t : 128 * t + 128]


def assemble_kernel(
    coords, qkv_own, out_own, up_own, b0, bx, by, bl, bh, d0, dx, dy, dl, dh, w_pairs, w_out, w_up
):
    depth_at, plane_at, core_at = coords[0], coords[1], coords[2]
    w_up[pl.ds(pl.multiple_of(depth_at * 96, 32), 96), :] = up_own[...]
    base = pl.multiple_of(depth_at * 192, 64)
    for part in range(3):
        for p in range(6):
            at = 768 * part + 128 * p
            w_pairs[p, pl.ds(base, 192), 128 * part : 128 * part + 128] = qkv_own[:, at : at + 128]
    w_out[pl.ds(base, 192), :] = out_own[...]
    for core, lows in ((core_at, (b0, bx, by, bl, bh)), (1 - core_at, (d0, dx, dy, dl, dh))):
        column = pl.multiple_of(core * 384, 128)
        tiles = [core * 9 + t for t in range(9)]
        pairs_at = [t % 6 for t in tiles]
        lanes_at = [pl.multiple_of(t // 6 * 128, 128) for t in tiles]
        for far in range(4):
            plane = plane_at ^ far
            for step in range(1, 4):
                shard = (depth_at + step) % 4
                row = pl.multiple_of(shard * 192 + plane * 48, 16)
                if far < 3:
                    left, right = lows[far].at[step - 1, :, 0:1152], lows[far].at[step - 1, :, 1152:1920]
                else:
                    left, right = lows[3].at[step - 1], lows[4].at[step - 1]
                for t in range(9):
                    w_pairs[pairs_at[t], pl.ds(row, 48), pl.ds(lanes_at[t], 128)] = left[:, 128 * t : 128 * t + 128]
                w_out[pl.ds(row, 48), pl.ds(column, 384)] = right[:, 0:384]

                @pl.when(plane < 3)
                def _():
                    for g in range(2):
                        up_row = pl.multiple_of(shard * 96 + plane * 32 + 16 * g, 16)
                        for t in range(3):
                            lane = 384 + 128 * g
                            to = pl.ds(pl.multiple_of(core * 384 + 128 * t, 128), 128)
                            w_up[pl.ds(up_row, 16), to] = right[16 * t : 16 * t + 16, lane : lane + 128]


def lookup_kernel(coords, ids, table_own, t0, tx, ty, tl, th, rows_own, rows_other, table, total):
    plane_at = coords[1]
    at = pl.program_id(0)

    @pl.when(at == 0)
    def _():
        table[...] = table_own[0]
        total[...] = jnp.zeros_like(total)

    for step in range(1, 4):
        @pl.when(at == step)
        def _():
            for far, ref in enumerate((t0, tx, ty)):
                table[pl.ds(pl.multiple_of((plane_at ^ far) * 48, 16), 48), :] = ref[step - 1]
            last = pl.ds(pl.multiple_of((plane_at ^ 3) * 48, 16), 48)
            table[last, 0:896] = tl[step - 1]
            table[last, 896:1792] = th[step - 1]

    wanted = ids[...] - at * 1792
    line = lax.broadcasted_iota(jnp.int32, (256, 1536), 0)
    part = jnp.zeros((192, 1536), F32)
    for chunk in range(7):
        hot = jnp.where(line + 256 * chunk == wanted, 1.0, 0.0).astype(BF16)
        part += mm(table[:, 256 * chunk : 256 * chunk + 256], hot)
    total[...] += part

    @pl.when(at == 3)
    def _():
        rows_own[...] = total[:, 0:768].astype(BF16)
        rows_other[...] = total[:, 768:1536].astype(BF16)


def project_kernel(
    coords, rows_own, rows_other, embedded, w_up, gain, w_pair, cosine, sine,
    residual, act_out, queries, keys, values, act,
):
    core_at = coords[2]

    @pl.when(pl.program_id(0) == 0)
    def _():
        first = pl.multiple_of(core_at * 192, 64)
        second = pl.multiple_of(192 - core_at * 192, 64)
        x = embedded[...].astype(F32)
        x += mm(rows_own[...], w_up[pl.ds(first, 192), :], TN)
        x += mm(rows_other[...], w_up[pl.ds(second, 192), :], TN)
        residual[...] = x
        inverse = lax.rsqrt(jnp.mean(x * x, axis=-1, keepdims=True) + norm_eps)
        low = (x * inverse * gain[...]).astype(BF16)
        act[...] = low
        act_out[...] = low

    projected = mm(act[...], w_pair[0])
    cos, sin = cosine[...], sine[...]
    q, k = projected[:, 0:128], projected[:, 128:256]
    queries[0] = ((q * cos + swap_halves(q) * sin) * 0.125).astype(BF16)
    keys[0] = (k * cos + swap_halves(k) * sin).astype(BF16)
    values[0] = projected[:, 256:384].astype(BF16)


def attend_kernel(last, coords, queries, keys, values, bias, residual, w_out, *rest):
    if last:
        gain, weights_out, attended, middle, act_two, total = rest
    else:
        weights_out, attended, total = rest
    pair = pl.program_id(0)
    lane = lax.broadcasted_iota(jnp.int32, (384, 128), 1)
    columns = []
    for seq in range(2):
        rows = slice(384 * seq, 384 * seq + 384)
        q, k = queries[0, rows, :], keys[0, rows, :]
        v = values[0, rows, :]
        heads = []
        for head in range(2):
            q_head = jnp.where((lane >= 64) == (head == 1), q, jnp.zeros_like(q))
            scores = mm(k, q_head, NT) + bias[seq]
            top = jnp.max(scores, axis=0, keepdims=True)
            raised = jnp.exp(scores - top)
            weight = (raised * (1.0 / jnp.sum(raised, axis=0, keepdims=True))).astype(BF16)
            weights_out[0, seq, head] = weight
            heads.append(mm(weight, jnp.where((lane >= 64) == (head == 1), v, jnp.zeros_like(v)), TN))
        columns.append(heads[0] + heads[1])
    low = jnp.concatenate(columns, axis=0).astype(BF16)
    attended[0] = low
    part = mm(low, w_out[...])

    @pl.when(pair == 0)
    def _():
        total[...] = residual[...] + part

    @pl.when(pair > 0)
    def _():
        total[...] += part

    if not last:
        return

    @pl.when(pair == 2)
    def _():
        mid = total[...]
        middle[...] = mid
        inverse = lax.rsqrt(jnp.mean(mid * mid, axis=-1, keepdims=True) + norm_eps)
        act_two[...] = (mid * inverse * gain[...]).astype(BF16)


def feed_kernel(half, coords, act, cotangent, gate_up_own, down_own, b0, bx, by, bd, d0, dx, dy, dd, *rest):
    if half == 0:
        total, grad_act, grads, w_gate_up, w_down = rest
    else:
        (total_in, grad_act_in, middle, gain, attended_a, attended_b,
         output, grads, grad_mid, grad_low, gain_grad, total, grad_act, w_gate_up, w_down) = rest
    depth_at, plane_at, core_at = coords[0], coords[1], coords[2]
    at = pl.program_id(0)

    def assemble():
        base = pl.multiple_of(depth_at * 192, 64)
        for part in range(2):
            for shard in range(4):
                start = 2048 * part + 512 * shard + 256 * half
                w_gate_up[part, pl.ds(base, 192), 256 * shard : 256 * shard + 256] = gate_up_own[:, start : start + 256]
        w_down[pl.ds(pl.multiple_of(depth_at * 256, 256), 256), :] = down_own[256 * half : 256 * half + 256, :]
        for core, lows in ((core_at, (b0, bx, by, bd)), (1 - core_at, (d0, dx, dy, dd))):
            for far in range(4):
                plane = plane_at ^ far
                for step in range(1, 4):
                    shard = (depth_at + step) % 4
                    row = pl.multiple_of(shard * 192 + plane * 48, 16)
                    piece = lows[far].at[step - 1]
                    w_gate_up[core, pl.ds(row, 48), :] = piece[:, 0:1024]
                    for g in range(4):
                        for t in range(3):
                            row = pl.multiple_of(shard * 256 + plane * 64 + 16 * g, 16)
                            column = pl.multiple_of(core * 384 + 128 * t, 128)
                            lane = 1024 + 128 * g
                            w_down[pl.ds(row, 16), pl.ds(column, 128)] = piece[16 * t : 16 * t + 16, lane : lane + 128]

    @pl.when(at == 0)
    def _():
        total[...] = total_in[...] if half else jnp.zeros_like(total)
        grad_act[...] = grad_act_in[...] if half else jnp.zeros_like(grad_act)
        assemble()

    second = at
    units = pl.ds(pl.multiple_of(second * 512, 512), 512)
    a, c = act[...], cotangent[...]
    w_g, w_u, w_d = w_gate_up[0, :, units], w_gate_up[1, :, units], w_down[units, :]
    gate = mm(a, w_g)
    up = mm(a, w_u)
    back = mm(c, w_d, NT)
    sig = 0.5 * jnp.tanh(0.5 * gate) + 0.5
    silu = gate * sig
    inner = (silu * up).astype(BF16)
    d_up = (back * silu).astype(BF16)
    d_gate = (back * up * (sig * (1.0 + gate * (1.0 - sig)))).astype(BF16)
    total[...] += mm(inner, w_d)
    grad_act[...] += mm(d_gate, w_g, NT) + mm(d_up, w_u, NT)
    gate_g = mm(a, d_gate, TN).astype(BF16)
    up_g = mm(a, d_up, TN).astype(BF16)
    down = mm(inner, c, TN).astype(BF16)
    lanes = pl.ds(pl.multiple_of(second * 512, 512), 512)
    for plane in range(4):
        for core in range(2):
            q = 2 * plane + core
            block = up_g if core else gate_g
            for shard in range(4):
                row = 192 * shard + 48 * plane
                grads[q, (shard + 4 - depth_at) % 4, :, lanes] = block[row : row + 48, :]
            for b in range(2):
                for g in range(4):
                    low_lanes = slice(1024 + 128 * g, 1152 + 128 * g)
                    for t in range(3):
                        row = 256 * b + 64 * plane + 16 * g
                        column = 384 * core + 128 * t
                        grads[q, (2 * second + b + 4 - depth_at) % 4, 16 * t : 16 * t + 16, low_lanes] = down[
                            row : row + 16, column : column + 128
                        ]

    if half == 0:
        return

    @pl.when(at == 1)
    def _():
        mid = middle[...]
        output[...] = (mid + total[...]).astype(BF16)
        inverse = lax.rsqrt(jnp.mean(mid * mid, axis=-1, keepdims=True) + norm_eps)
        normed = mid * inverse
        grad = grad_act[...]
        gain_grad[...] = jnp.sum(grad * normed, axis=0, keepdims=True)
        n = grad * gain[...]
        g = cotangent[...].astype(F32) + inverse * (n - normed * jnp.mean(n * normed, axis=-1, keepdims=True))
        grad_mid[...] = g
        low = g.astype(BF16)
        grad_low[...] = low
        out_g = [mm(attended[p], low, TN) for attended in (attended_a, attended_b) for p in range(3)]
        out_g = jnp.concatenate(out_g, axis=0).astype(BF16)
        for plane in range(4):
            for core in range(2):
                for shard in range(4):
                    row = 192 * shard + 48 * plane
                    grads[2 * plane + core, (shard + 4 - depth_at) % 4, :, 1536:1920] = out_g[row : row + 48, 384 * core : 384 * core + 384]


def second_half_kernel(
    coords, queries, keys, values, weights_a, weights_b, grad_low, w_out, w_pair, cosine, sine,
    w_up, residual, grad_mid, gain,
    embedding_grad, grad_projected, rows_kept, rows_sent, gain_grad, grad_act,
):
    depth_at, plane_at, core_at = coords[0], coords[1], coords[2]
    step = pl.program_id(0)
    lane = lax.broadcasted_iota(jnp.int32, (384, 128), 1)

    @pl.when(step == 0)
    def _():
        grad_act[...] = jnp.zeros_like(grad_act)

    grad_attended = mm(grad_low[...], w_out[...], NT).astype(BF16)
    threes = []
    for seq in range(2):
        rows = slice(384 * seq, 384 * seq + 384)
        q, k, v, ga = queries[0, rows, :], keys[0, rows, :], values[0, rows, :], grad_attended[rows, :]
        grad_q = jnp.zeros((384, 128), F32)
        grad_k = jnp.zeros((384, 128), F32)
        grad_v = jnp.zeros((384, 128), F32)
        for head in range(2):
            mine = (lane >= 64) == (head == 1)
            ga_head = jnp.where(mine, ga, jnp.zeros_like(ga))
            q_head = jnp.where(mine, q, jnp.zeros_like(q))
            weight_low = jnp.where(step < 3, weights_a[0, seq, head], weights_b[0, seq, head])
            weight = weight_low.astype(F32)
            grad_weight = mm(v, ga_head, NT)
            row = jnp.sum(grad_weight * weight, axis=0, keepdims=True)
            grad_scores = (weight * (grad_weight - row)).astype(BF16)
            grad_v += mm(weight_low, ga_head)
            grad_k += mm(grad_scores, q_head)
            grad_q += mm(grad_scores, jnp.where(mine, k, jnp.zeros_like(k)), TN)
        grad_q = grad_q * 0.125
        cos, sin = cosine[rows, :], sine[rows, :]
        grad_q = (grad_q * cos - swap_halves(grad_q) * sin).astype(BF16)
        grad_k = (grad_k * cos - swap_halves(grad_k) * sin).astype(BF16)
        threes.append(jnp.concatenate([grad_q, grad_k, grad_v.astype(BF16)], axis=1))
    three = jnp.concatenate(threes, axis=0)
    grad_act[...] += mm(three, w_pair[0], NT)
    grad_projected[0] = three

    @pl.when(step == 5)
    def _():
        grad = grad_act[...]
        x = residual[...]
        inverse = lax.rsqrt(jnp.mean(x * x, axis=-1, keepdims=True) + norm_eps)
        normed = x * inverse
        gain_grad[...] = jnp.sum(grad * normed, axis=0, keepdims=True)
        n = grad * gain[...]
        g = grad_mid[...] + inverse * (n - normed * jnp.mean(n * normed, axis=-1, keepdims=True))
        low = g.astype(BF16)
        embedding_grad[...] = low
        rows = mm(w_up[...], low, NT).astype(BF16)

        @pl.when(core_at == 0)
        def _():
            rows_kept[...] = rows[0:192]
            rows_sent[...] = rows[192:384]

        @pl.when(core_at == 1)
        def _():
            rows_kept[...] = rows[192:384]
            rows_sent[...] = rows[0:192]


def both_ways(core_at, kept, sent, place):
    @pl.when(core_at == 0)
    def _():
        place(0, kept)
        place(1, sent)

    @pl.when(core_at == 1)
    def _():
        place(1, kept)
        place(0, sent)


def weight_grad_kernel(coords, act, grad_projected, kept, sent):
    depth_at, plane_at, core_at = coords[0], coords[1], coords[2]
    step = pl.program_id(0)
    weight_g = mm(act[...], grad_projected[0], TN)

    def place(core, out):
        for part in range(3):
            lanes = pl.ds(pl.multiple_of(512 + 768 * part + step * 128, 128), 128)
            for plane in range(4):
                for shard in range(4):
                    row = 192 * shard + 96 * core + 24 * plane
                    out[(shard + 4 - depth_at) % 4, plane ^ plane_at, :, lanes] = weight_g[
                        row : row + 24, 128 * part : 128 * part + 128
                    ].astype(BF16)

    both_ways(core_at, kept, sent, place)


def up_grad_kernel(
    coords, kept_in, sent_in, rows_own, rows_other, embedding_grad, gain_one_grad, gain_two_grad, kept, sent
):
    depth_at, plane_at, core_at = coords[0], coords[1], coords[2]
    low = embedding_grad[...]
    mine, other = mm(rows_own[...], low), mm(rows_other[...], low)
    first = jnp.where(core_at == 0, mine, other)
    second = jnp.where(core_at == 0, other, mine)
    both = jnp.concatenate([first, second], axis=0)
    one, two = gain_one_grad[...], gain_two_grad[...]

    def place(core, out):
        for plane in range(4):
            for shard in range(4):
                row = 96 * shard + 24 * plane
                far, near = (shard + 4 - depth_at) % 4, plane ^ plane_at
                out[far, near, :, 0:384] = both[row : row + 24, 384 * core : 384 * core + 384].astype(BF16)
                lines = jnp.zeros((24, 128), F32)
                if core == 0 and plane == 0:
                    start = 192 * shard
                    line = jnp.concatenate([one[:, start : start + 192], two[:, start : start + 192]], axis=1)
                    lines = jnp.concatenate(
                        [line[:, 0:128], line[:, 128:256], line[:, 256:384], jnp.zeros((21, 128), F32)], axis=0
                    )
                out[far, near, :, 384:512] = lines.astype(BF16)

    both_ways(core_at, kept, sent, place)


def table_add(ids, ref, total):
    line = lax.broadcasted_iota(jnp.int32, (2048, 768), 0)
    hot = jnp.where(line == ids[0], 1.0, 0.0).astype(BF16)
    total[...] += mm(ref[0] if len(ref.shape) == 3 else ref[...], hot, NT)


def table_kernel(sources, first, coords, ids, *rest):
    refs = rest[:sources]
    total = rest[-1]
    at = pl.program_id(0)

    @pl.when(at == 0)
    def _():
        total[...] = jnp.zeros_like(total) if first else rest[sources][...]

    for source, ref in enumerate(refs):
        @pl.when(at == source)
        def _():
            table_add(ids, ref, total)


def table_last_kernel(coords, ids, low, high, before, kept_x, kept_y, got_y, got_x, *rest):
    outs, total = rest[:4], rest[4]
    at = pl.program_id(0)

    @pl.when(at == 0)
    def _():
        total[...] = before[...]
        table_add(ids, low, total)
        for i in range(2):
            outs[i][:, 0:2816] = (kept_x[i].astype(F32) + got_y[i].astype(F32)).astype(BF16)
            outs[i + 2][:, 0:2816] = (kept_y[i].astype(F32) + got_x[i].astype(F32)).astype(BF16)

    @pl.when(at == 1)
    def _():
        table_add(ids, high, total)
        for shard in range(4):
            for g in range(8):
                lane = 2816 + 512 * g
                outs[shard][:, lane : lane + 512] = total[24 * g : 24 * g + 24, 512 * shard : 512 * shard + 512].astype(BF16)


def add_kernel(coords, *refs):
    total = refs[0][...].astype(F32)
    for ref in refs[1:-1]:
        total = total + ref[...].astype(F32)
    refs[-1][...] = total.astype(BF16)


def join_kernel(coords, first, *refs):
    refs[-1][:, 0:1536] = first[...]
    total = refs[0][...].astype(F32)
    for ref in refs[1:-1]:
        total = total + ref[...].astype(F32)
    refs[-1][:, 1536:3456] = total.astype(BF16)


def add_all(coords, parts, after=()):
    shape = parts[0].shape
    return kernel_call(
        add_kernel, coords, parts, [full(shape)] * len(parts), [sds(shape, BF16)], [full(shape)], (1,),
        micros=1.5, vmem=16, name="add", after=after,
    )[0]


def split_kernel(coords, value, *parts):
    for at, part in enumerate(parts):
        part[...] = value[0, at]


def first_sum_kernel(coords, kept, got, send_x, send_y, keep_x, keep_y):
    for shard in range(4):
        for plane in range(4):
            value = (kept[shard, plane].astype(F32) + got[shard, plane].astype(F32)).astype(BF16)
            if shard < 2:
                (send_x if plane % 2 else keep_x)[shard, plane // 2] = value
            else:
                (send_y if plane // 2 else keep_y)[shard - 2, plane % 2] = value


def second_sum_kernel(coords, keep_x, keep_y, got_x, got_y, send_y, send_x, kept_x, kept_y):
    for i in range(2):
        send_y[i] = (keep_x[i, 1].astype(F32) + got_x[i, 1].astype(F32)).astype(BF16)
        send_x[i] = (keep_y[i, 1].astype(F32) + got_y[i, 1].astype(F32)).astype(BF16)
        kept_x[i] = (keep_x[i, 0].astype(F32) + got_x[i, 0].astype(F32)).astype(BF16)
        kept_y[i] = (keep_y[i, 0].astype(F32) + got_y[i, 0].astype(F32)).astype(BF16)


def each_piece(coords, refs):
    for index, ref in enumerate(refs):
        yield coords[2] ^ (index // 4), coords[1] ^ (index % 4), ref


def finish_feed_kernel(coords, *refs):
    gate_up, down, out = refs[8:]
    for core, plane, ref in each_piece(coords, refs[0:8]):
        rows = pl.ds(pl.multiple_of(plane * 48, 16), 48)
        for half in range(2):
            for j in range(4):
                lanes = pl.ds(pl.multiple_of(core * 2048 + 512 * j + 256 * half, 256), 256)
                at = 1536 * half + 256 * j
                gate_up[rows, lanes] = ref[:, at : at + 256].astype(F32)
            for g in range(4):
                for t in range(3):
                    low_rows = pl.ds(pl.multiple_of(256 * half + plane * 64 + 16 * g, 16), 16)
                    lanes = pl.ds(pl.multiple_of(core * 384 + 128 * t, 128), 128)
                    at = 1536 * half + 1024 + 128 * g
                    down[low_rows, lanes] = ref[16 * t : 16 * t + 16, at : at + 128].astype(F32)
        out[rows, pl.ds(pl.multiple_of(core * 384, 128), 384)] = ref[:, 3072:3456].astype(F32)


def finish_rest_kernel(coords, *refs):
    qkv, up, gains, table = refs[8:]
    for core, plane, ref in each_piece(coords, refs[0:8]):
        rows = pl.ds(pl.multiple_of(core * 96 + plane * 24, 8), 24)
        qkv[rows, :] = ref[:, 512:2816].astype(F32)
        up_rows = pl.ds(pl.multiple_of(plane * 24, 8), 24)
        up[up_rows, pl.ds(pl.multiple_of(core * 384, 128), 384)] = ref[:, 0:384].astype(F32)
        for g in range(8):
            lane = 2816 + 512 * g
            at = pl.ds(pl.multiple_of(plane * 512, 512), 256)
            table[core, 24 * g : 24 * g + 24, at] = ref[:, lane : lane + 256].astype(F32)

        @pl.when(plane < 3)
        def _():
            for g in range(8):
                lane = 2816 + 512 * g + 256
                at = pl.ds(pl.multiple_of(plane * 512 + 256, 256), 256)
                table[core, 24 * g : 24 * g + 24, at] = ref[:, lane : lane + 256].astype(F32)

        @pl.when((core == 0) & (plane == 0))
        def _():
            value = ref[:, 384:512].astype(F32)
            line = jnp.concatenate([value[i : i + 1] for i in range(3)], axis=1)
            gains[0:1, :] = line[:, 0:192]
            gains[1:2, :] = line[:, 192:384]


def rotary_lanes(segments):
    seq_len = segments.shape[-1]
    position = jnp.arange(seq_len, dtype=jnp.int32)
    same = segments[:, :, None] == segments[:, None, :]
    start = jnp.min(jnp.where(same, position[None, None, :], seq_len), axis=-1)
    offset = (position[None, :] - start).astype(F32)
    half = HEAD_DIM // 2
    frequency = theta_base ** (-jnp.arange(half, dtype=F32) / half)
    angle = offset[..., None] * frequency
    cos, sin = jnp.cos(angle), jnp.sin(angle)
    cosine = jnp.concatenate([cos, cos, cos, cos], axis=-1)
    sine = jnp.concatenate([-sin, sin, -sin, sin], axis=-1)
    return cosine.reshape(-1, 128), sine.reshape(-1, 128), same


def body(
    sizes, embedded, cotangent, ngram_ids, segments, live_mask, tables, w_qkv, w_out, w_gate_up, w_down, up_proj, norm_gains
):
    depth, groups = sizes
    micro, _, seq, width = embedded.shape
    tokens = micro * seq
    rows_dev = tables.shape[1]
    depth_at = lax.axis_index("fsdp")
    octet = lax.axis_index("oct")
    core_at = octet & 1
    plane_at = octet >> 1
    coords = jnp.stack([depth_at, plane_at, core_at]).astype(jnp.int32)
    embedded = embedded.reshape(tokens, width)
    cotangent = cotangent.reshape(tokens, width)
    segments = segments.reshape(micro, seq)
    live_mask = live_mask.reshape(micro, seq)
    ids = ngram_ids.reshape(2, tokens)
    tables_t = jnp.transpose(tables, (0, 2, 1))

    gain_block = jnp.pad(norm_gains.reshape(3, 128), ((0, 45), (0, 0)))
    (top,) = kernel_call(
        prepare_table_kernel,
        coords,
        [tables_t],
        [pl.BlockSpec((1, 48, rows_dev), lambda i, at: (at[2], at[1], 0))],
        [sds((48, rows_dev), BF16)],
        [full((48, rows_dev))],
        (1,),
        micros=1,
        name="prepare_table",
    )
    top_held = stack(coords, along_depth(top, depth))
    top_x, top_y = by_x(top_held), by_y(top_held)
    (low,) = kernel_call(
        prepare_low_kernel,
        coords,
        [w_qkv, w_out, up_proj, gain_block],
        [
            pl.BlockSpec((48, 1152), lambda i, at: (at[1], at[2])),
            pl.BlockSpec((48, 384), lambda i, at: (at[1], at[2])),
            pl.BlockSpec((32, 384), lambda i, at: (jnp.minimum(at[1], 2), at[2])),
            full((48, 128)),
        ],
        [sds((48, 1920), BF16)],
        [full((48, 1920))],
        (1,),
        micros=1,
        name="prepare_low",
        after=[top_held],
    )
    low_steps = along_depth(low, depth)
    top_low, top_high = cut_pieces(coords, top_x, top_y, 896)
    low_held = stack(coords, low_steps, after=[top_low])
    low_x, low_y = by_x(low_held), by_y(low_held)
    tops = [top_held, top_x, top_y, by_y(top_low), by_x(top_high)]
    (feed,) = kernel_call(
        prepare_feed_kernel,
        coords,
        [w_gate_up, w_down, w_down],
        [
            pl.BlockSpec((48, 2048), lambda i, at: (at[1], at[2])),
            pl.BlockSpec((64, 384), lambda i, at: (at[1], at[2])),
            pl.BlockSpec((64, 384), lambda i, at: (4 + at[1], at[2])),
        ],
        [sds((48, 3072), BF16)],
        [full((48, 3072))],
        (1,),
        micros=1,
        name="prepare_feed",
        after=[low_held],
    )

    feed_steps = along_depth(feed, depth)

    gains_rel = jnp.concatenate([norm_gains[None], low_held[:, 0:3, 1792:1920].reshape(depth - 1, 2, 192)], axis=0)
    gains = jnp.roll(gains_rel, depth_at, axis=0).transpose(1, 0, 2).reshape(2, width).astype(F32)
    gain_one, gain_two = gains[0:1], gains[1:2]

    ids_other = by_core(ids)
    wanted = jnp.concatenate(
        [
            lax.dynamic_index_in_dim(ids, core_at, axis=0),
            lax.dynamic_index_in_dim(ids_other, core_at, axis=0),
        ],
        axis=0,
    )
    shard = wanted // rows_dev
    inside = wanted - shard * rows_dev
    line = ((shard - depth_at) % depth) * rows_dev + inside
    rows_own, rows_sent = kernel_call(
        lookup_kernel,
        coords,
        [line.reshape(1, 2 * tokens), tables_t] + list(tops),
        [full((1, 2 * tokens)), pl.BlockSpec((1, 192, rows_dev), lambda i, at: (at[2], 0, 0))] + [full(t.shape) for t in tops],
        [sds((192, tokens), BF16)] * 2,
        [full((192, tokens))] * 2,
        (4,),
        scratch=[pltpu.VMEM((192, rows_dev), BF16), pltpu.VMEM((192, 2 * tokens), F32)],
        micros=8,
        name="lookup",
        after=[low_held, feed],
    )
    rows_other = by_core(rows_sent)

    low_low, low_high = cut_pieces(coords, low_x, low_y, 1152, after=[rows_sent])
    lows = [low_held, low_x, low_y, by_y(low_low), by_x(low_high)]
    gathered = lows + [by_core(piece) for piece in lows]
    feed_held = stack(coords, feed_steps, after=[low_low])
    feed_x, feed_y = by_x(feed_held), by_y(feed_held)
    w_pairs, w_out_full, w_up_full = kernel_call(
        assemble_kernel,
        coords,
        [w_qkv, w_out, up_proj] + gathered,
        [full(a.shape) for a in [w_qkv, w_out, up_proj] + gathered],
        [sds((6, width, 384), BF16), sds((width, width), BF16), sds((384, width), BF16)],
        [full((6, width, 384)), full((width, width)), full((384, width))],
        (1,),
        vmem=32,
        name="assemble",
        after=[feed_held],
    )

    near = jnp.stack([wanted, by_x(wanted)])
    plane_ids = jnp.concatenate([near, by_y(near)], axis=0)
    t_shard = plane_ids // rows_dev
    t_inside = plane_ids - t_shard * rows_dev
    target = jnp.where(
        t_inside // 512 == plane_at, ((t_shard - depth_at) % depth) * 512 + t_inside % 512, -1
    ).reshape(8, 1, tokens)

    cosine, sine, same = rotary_lanes(segments)
    position = jnp.arange(seq, dtype=jnp.int32)
    usable = same & (position[None, :, None] <= position[None, None, :]) & (live_mask[:, :, None] == 1)
    usable = usable | (position[None, :, None] == position[None, None, :])
    bias = jnp.where(usable, 0.0, masked_score).astype(F32)

    whole = full((tokens, width))
    line_spec = full((1, width))
    turn = full((tokens, 128))

    def pair_block(start):
        return pl.BlockSpec((1, tokens, 128), lambda p, *_: (p + start, 0, 0))

    residual, act_one, queries, keys, values = kernel_call(
        project_kernel,
        coords,
        [rows_own, rows_other, embedded, w_up_full, gain_one, w_pairs, cosine, sine],
        [full((192, tokens))] * 2
        + [whole, full((384, width)), line_spec, pl.BlockSpec((1, width, 384), lambda p, *_: (p, 0, 0)), turn, turn],
        [sds((tokens, width), F32), sds((tokens, width), BF16)] + [sds((6, tokens, 128), BF16)] * 3,
        [whole, whole] + [pair_block(0)] * 3,
        (6,),
        scratch=[pltpu.VMEM((tokens, width), BF16)],
        micros=12,
        vmem=36,
        name="project",
        after=[target],
    )

    def attend_call(start, before, extra, extra_specs, outs, out_specs, after):
        return kernel_call(
            lambda *refs: attend_kernel(start > 0, *refs),
            coords,
            [queries, keys, values, bias, before, w_out_full] + extra,
            [pair_block(start)] * 3
            + [full((micro, seq, seq)), whole, pl.BlockSpec((128, width), lambda p, *_: (p + start, 0))] + extra_specs,
            [sds((3, micro, 2, seq, seq), BF16), sds((3, tokens, 128), BF16)] + outs,
            [pl.BlockSpec((1, micro, 2, seq, seq), lambda p, *_: (p, 0, 0, 0, 0)),
             pair_block(0)] + out_specs,
            (3,),
            scratch=[pltpu.VMEM((tokens, width), F32)] if start else [],
            micros=12,
            name="attend",
            after=after,
        )

    feed_low, feed_high = cut_pieces(coords, feed_x, feed_y, 1536, after=[queries])
    feed_low, feed_high = by_y(feed_low), by_x(feed_high)
    weights_a, attended_a, partial = attend_call(0, residual, [], [], [sds((tokens, width), F32)], [whole], [])
    weights_b, attended_b, middle, act_two = attend_call(
        3, partial, [gain_two], [line_spec],
        [sds((tokens, width), F32), sds((tokens, width), BF16)], [whole, whole],
        [feed_low, feed_high],
    )
    wholes = [feed_held, feed_x, feed_y]
    others = [by_core(piece) for piece in wholes]
    feed_parts = [wholes + [feed_low] + others + [by_core(feed_low)], wholes + [feed_high] + others + [by_core(feed_high)]]

    def single(shape):
        return pl.BlockSpec(shape, lambda *_: (0,) * len(shape), pipeline_mode=pl.Buffered(1))

    one = single((tokens, width))
    feed_scratch = [pltpu.VMEM((2, width, 1024), BF16), pltpu.VMEM((1024, width), BF16)]

    def feed_specs(half):
        part = pl.BlockSpec((depth - 1, 48, 1536), lambda *_: (0, 0, half), pipeline_mode=pl.Buffered(1))
        return [one, one, single(w_gate_up.shape), single(w_down.shape)] + ([part] * 3 + [single((depth - 1, 48, 1536))]) * 2

    feed_in = [act_two, cotangent, w_gate_up, w_down]
    grads_shapes = [(8, depth, 48, 1536), (8, depth, 48, 1920)]
    total, grad_act, feed_grads = kernel_call(
        lambda *refs: feed_kernel(0, *refs),
        coords,
        feed_in + feed_parts[0],
        feed_specs(0),
        [sds((tokens, width), F32), sds((tokens, width), F32), sds(grads_shapes[0], BF16)],
        [one, one, single(grads_shapes[0])],
        (2,),
        scratch=feed_scratch,
        micros=20,
        name="feed_first",
    )
    feed_part_a = lax.psum_scatter(feed_grads, "oct", scatter_dimension=0, tiled=True)
    output, feed_grads, grad_mid, grad_low, gain_two_grad = kernel_call(
        lambda *refs: feed_kernel(1, *refs),
        coords,
        feed_in + feed_parts[1] + [total, grad_act, middle, gain_two, attended_a, attended_b],
        feed_specs(1) + [one, one, one, line_spec] + [single((3, tokens, 128))] * 2,
        [sds((tokens, width), BF16), sds(grads_shapes[1], BF16), sds((tokens, width), F32), sds((tokens, width), BF16),
         sds((1, width), F32)],
        [one, single(grads_shapes[1]), one, one, line_spec],
        (2,),
        scratch=[pltpu.VMEM((tokens, width), F32)] * 2 + feed_scratch,
        micros=24,
        name="feed_second",
    )
    feed_part_b = lax.psum_scatter(feed_grads, "oct", scatter_dimension=0, tiled=True)

    def steps_block(shape, place):
        return pl.BlockSpec(shape, lambda p, *_: place(p) + (0,) * (len(shape) - 1))

    tail_shape = sds((4, 4, 24, 2816), BF16)
    weights_shape = (1, micro, 2, seq, seq)
    embedding_grad, grad_projected, rows_kept, rows_sent, gain_one_grad = kernel_call(
        second_half_kernel,
        coords,
        [queries, keys, values, weights_a, weights_b, grad_low, w_out_full, w_pairs, cosine, sine, w_up_full, residual,
         grad_mid, gain_one],
        [pair_block(0)] * 3
        + [steps_block(weights_shape, lambda p: (jnp.minimum(p, 2),)), steps_block(weights_shape, lambda p: (jnp.maximum(p - 3, 0),)),
           whole, pl.BlockSpec((128, width), lambda p, *_: (p, 0)), pl.BlockSpec((1, width, 384), lambda p, *_: (p, 0, 0)),
           turn, turn, full((384, width)), whole, whole, line_spec],
        [sds((tokens, width), BF16), sds((6, tokens, 384), BF16), sds((192, tokens), BF16), sds((192, tokens), BF16),
         sds((1, width), F32)],
        [whole, pl.BlockSpec((1, tokens, 384), lambda p, *_: (p, 0, 0)), full((192, tokens)), full((192, tokens)), line_spec],
        (6,),
        scratch=[pltpu.VMEM((tokens, width), F32)],
        micros=36,
        name="second_half",
    )

    rows_got = by_core(rows_sent)
    held = stack(coords, [rows_kept, rows_got])
    held_x, held_y = by_x(held), by_y(held)
    kept_c, sent_c = kernel_call(
        weight_grad_kernel,
        coords,
        [act_one, grad_projected],
        [whole, pl.BlockSpec((1, tokens, 384), lambda p, *_: (p, 0, 0))],
        [tail_shape, tail_shape],
        [full(tail_shape.shape)] * 2,
        (6,),
        micros=9,
        name="weight_grad",
        after=[held],
    )

    def split_call(part, after):
        shape = part.shape[2:]
        shards = kernel_call(
            split_kernel, coords, [part], [full(part.shape)], [sds(shape, BF16)] * depth, [full(shape)] * depth,
            (1,), micros=2, vmem=16, name="split", after=after,
        )
        return [shards[0]] + [to_ahead(shards[step], step, depth) for step in range(1, depth)]

    held_low, held_high = held_x[0], held_y[1]
    up_block = pl.BlockSpec((4, 4, 24, 512), lambda *_: (0, 0, 0, 0))
    kept_c, sent_c = kernel_call(
        up_grad_kernel,
        coords,
        [kept_c, sent_c, rows_own, rows_other, embedding_grad, gain_one_grad, gain_two_grad],
        [pl.BlockSpec(memory_space=pl.ANY)] * 2
        + [full((192, tokens)), full((192, tokens)), whole, line_spec, line_spec],
        [tail_shape, tail_shape],
        [up_block, up_block],
        (1,),
        micros=3,
        vmem=24,
        name="up_grad",
        after=[held_low, held_high],
        aliases=[(0, 0), (1, 1)],
    )
    held_low, held_high = by_y(held_low), by_x(held_high)
    got_c = by_core(sent_c)

    part_shape, low_shape = (2, 2, 24, 2816), (2, 24, 2816)
    send_x, send_y, keep_x, keep_y = kernel_call(
        first_sum_kernel, coords, [kept_c, got_c], [full(tail_shape.shape)] * 2, [sds(part_shape, BF16)] * 4,
        [full(part_shape)] * 4, (1,), micros=3, vmem=24, name="first_sum",
    )
    c_x, c_y = by_x(send_x), by_y(send_y)
    feed_got_a = split_call(feed_part_a, [send_x])

    def table_call(sources, refs, places, before, after):
        specs = [pl.BlockSpec((1, 192, tokens), lambda i, *_, place=place: (place, 0, 0)) for place in places]
        return kernel_call(
            lambda *r: table_kernel(len(refs), before is None, *r),
            coords,
            [target[sources]] + refs + ([] if before is None else [before]),
            [pl.BlockSpec((1, 1, tokens), lambda i, *_: (i, 0, 0))] + specs + ([] if before is None else [full((192, 2048))]),
            [sds((192, 2048), F32)],
            [full((192, 2048))],
            (len(refs),),
            micros=3 + len(refs),
            vmem=24,
        name="table_sum",
            after=after,
        )[0]

    sums = table_call(slice(0, 2), [held, held], [0, 1], None, [send_x])
    feed_sum_a = add_all(coords, feed_got_a, [send_x])
    send_y, send_x, kept_x, kept_y = kernel_call(
        second_sum_kernel, coords, [keep_x, keep_y, c_x, c_y], [full(part_shape)] * 4, [sds(low_shape, BF16)] * 4,
        [full(low_shape)] * 4, (1,), micros=2, vmem=16, name="second_sum", after=[feed_sum_a],
    )
    c_y, c_x = by_y(send_y), by_x(send_x)
    feed_got_b = split_call(feed_part_b, [send_y])
    sums = table_call(slice(2, 6), [held_x, held_x, held_y, held_y], [0, 1, 0, 1], sums, [feed_got_b[0]])
    shard_shape = (24, 6912)
    shards = kernel_call(
        table_last_kernel,
        coords,
        [target[6:8], held_low, held_high, sums, kept_x, kept_y, c_y, c_x],
        [pl.BlockSpec((1, 1, tokens), lambda i, *_: (i, 0, 0))] + [full((192, tokens))] * 2 + [full((192, 2048))]
        + [full(low_shape)] * 4,
        [sds(shard_shape, BF16)] * 4,
        [full(shard_shape)] * 4,
        (2,),
        scratch=[pltpu.VMEM((192, 2048), F32)],
        micros=6,
        vmem=24,
        name="table_last",
    )
    tail_got = [shards[0]] + [to_ahead(shards[step], step, depth) for step in range(1, depth)]
    pieces = spread(over_groups(add_all(coords, tail_got), groups))
    feed_sum = kernel_call(
        join_kernel, coords, [feed_sum_a] + feed_got_b, [full((48, 1536))] + [full((48, 1920))] * 4, [sds((48, 3456), BF16)],
        [full((48, 3456))], (1,), micros=2, vmem=16, name="join", after=[shards[0]],
    )[0]
    feed_pieces = spread(over_groups(feed_sum, groups))

    def finish(kernel, refs, outs, name):
        return kernel_call(
            kernel, coords, refs, [full(r.shape) for r in refs], outs, [full(o.shape) for o in outs], (1,), vmem=32, name=name
        )

    gate_up_grad, down_grad, out_grad = finish(
        finish_feed_kernel,
        feed_pieces,
        [sds((192, 4096), F32), sds((512, width), F32), sds((192, width), F32)],
        "finish_feed",
    )
    qkv_grad, up_grad, gains_grad, table_grad = finish(
        finish_rest_kernel,
        pieces,
        [sds((192, 2304), F32), sds((96, width), F32), sds((2, 192), F32), sds((2, 192, rows_dev), F32)],
        "finish_rest",
    )
    return (
        output.reshape(micro, 1, seq, width),
        embedding_grad.reshape(micro, 1, seq, width),
        jnp.transpose(table_grad, (0, 2, 1)),
        qkv_grad,
        out_grad,
        gate_up_grad,
        down_grad,
        up_grad,
        gains_grad,
    )


def solution(mesh):
    depth, rep = mesh.devices.shape
    groups = rep // 8
    fine = Mesh(mesh.devices.reshape(depth, groups, 8), ("fsdp", "grp", "oct"))
    every = ("fsdp", "grp", "oct")
    in_specs = (
        P(None, every, None, None),
        P(None, every, None, None),
        P(None, None, every, None),
        P(None, every, None),
        P(None, every, None),
        P(None, "fsdp", None),
        P("fsdp", None),
        P("fsdp", None),
        P("fsdp", None),
        P("fsdp", None),
        P("fsdp", None),
        P(None, "fsdp"),
    )
    out_specs = (
        P(None, every, None, None),
        P(None, every, None, None),
        P(None, "fsdp", None),
        P("fsdp", None),
        P("fsdp", None),
        P("fsdp", None),
        P("fsdp", None),
        P("fsdp", None),
        P(None, "fsdp"),
    )

    def step(*args):
        return body((depth, groups), *args)

    return jax.shard_map(step, mesh=fine, in_specs=in_specs, out_specs=out_specs, check_vma=False)
```

```python
import jax
import jax.numpy as jnp
import numpy as np
from jax import lax
from jax.experimental import pallas as pl
from jax.experimental.pallas import tpu as pltpu
from jax.sharding import Mesh, PartitionSpec as P

BF16 = jnp.bfloat16
F32 = jnp.float32
HEADS = 12
HEAD_DIM = 64
norm_eps = 1e-05
theta_base = 10000.0
masked_score = -1e30
MIB = 1 << 20

NN = (((1,), (0,)), ((), ()))
NT = (((1,), (1,)), ((), ()))
TN = (((0,), (0,)), ((), ()))


def mm(left, right, dims=NN):
    return lax.dot_general(left, right, dims, preferred_element_type=F32)


def sds(shape, dtype):
    return jax.ShapeDtypeStruct(shape, dtype)


def full(shape):
    return pl.BlockSpec(shape, lambda *_: (0,) * len(shape))


def kernel_call(
    kernel, coords, args, in_specs, out_shape, out_specs, grid, scratch=(), micros=5, vmem=60, name=None, after=(), aliases=()
):
    held = len(after)
    extra = [pl.BlockSpec(memory_space=pl.ANY)] * held

    def run(coords, *refs):
        kernel(coords, *refs[held:])

    return pl.pallas_call(
        run,
        out_shape=out_shape,
        grid_spec=pltpu.PrefetchScalarGridSpec(
            num_scalar_prefetch=1,
            grid=grid,
            in_specs=extra + list(in_specs),
            out_specs=out_specs,
            scratch_shapes=list(scratch),
        ),
        compiler_params=pltpu.CompilerParams(vmem_limit_bytes=vmem * MIB),
        input_output_aliases={1 + held + source: out for source, out in aliases},
        cost_estimate=pl.CostEstimate(flops=int(micros * 1.15e9), bytes_accessed=0, transcendentals=0),
        name=name,
    )(coords, *after, *args)


def by_core(value):
    return lax.ppermute(value, "oct", [(i, i ^ 1) for i in range(8)])


def by_x(value):
    return lax.ppermute(value, "oct", [(i, i ^ 2) for i in range(8)])


def by_y(value):
    return lax.ppermute(value, "oct", [(i, i ^ 4) for i in range(8)])


def from_ahead(value, step, size):
    return lax.ppermute(value, "fsdp", [((i + step) % size, i) for i in range(size)])


def to_ahead(value, step, size):
    return lax.ppermute(value, "fsdp", [(i, (i + step) % size) for i in range(size)])


def stack_kernel(coords, *refs):
    for at, ref in enumerate(refs[:-1]):
        refs[-1][at] = ref[...]


def cut_kernel(cut, coords, from_x, from_y, low, high):
    low[...] = from_x[:, :, 0:cut]
    high[...] = from_y[:, :, cut:]


def stack(coords, parts, after=()):
    shape = (len(parts),) + parts[0].shape
    return kernel_call(
        stack_kernel, coords, parts, [full(p.shape) for p in parts], [sds(shape, BF16)], [full(shape)], (1,),
        micros=1.5, vmem=16, name="stack", after=after,
    )[0]


def cut_pieces(coords, from_x, from_y, cut, after=()):
    shapes = [from_x.shape[:2] + (cut,), from_x.shape[:2] + (from_x.shape[2] - cut,)]
    return kernel_call(
        lambda *refs: cut_kernel(cut, *refs), coords, [from_x, from_y], [full(from_x.shape)] * 2,
        [sds(shape, BF16) for shape in shapes], [full(shape) for shape in shapes], (1,),
        micros=1.5, vmem=16, name="cut", after=after,
    )


def along_depth(piece, depth):
    return [from_ahead(piece, step, depth) for step in range(1, depth)]


def over_groups(value, groups):
    if groups > 1:
        value = lax.psum(value.astype(F32), "grp").astype(BF16)
    return value


def spread(value):
    from_x = by_x(value)
    four = [value, from_x, by_y(value), by_y(from_x)]
    return four + [by_core(piece) for piece in four]


def swap_halves(values):
    lane = lax.broadcasted_iota(jnp.int32, values.shape, 1)
    return jnp.where((lane & 63) < 32, pltpu.roll(values, 96, 1), pltpu.roll(values, 32, 1))


def prepare_table_kernel(coords, table, top):
    top[...] = table[0]


def prepare_low_kernel(coords, qkv, out, up, gains, low):
    low[:, 0:1152] = qkv[...]
    low[:, 1152:1536] = out[...]
    for g in range(2):
        for t in range(3):
            lane = 1536 + 128 * g
            low[16 * t : 16 * t + 16, lane : lane + 128] = up[16 * g : 16 * g + 16, 128 * t : 128 * t + 128]
    low[:, 1792:1920] = gains[...]


def prepare_feed_kernel(coords, gate_up, down_a, down_b, feed):
    for half, down in enumerate((down_a, down_b)):
        for shard in range(4):
            start = 512 * shard + 256 * half
            at = 1536 * half + 256 * shard
            feed[:, at : at + 256] = gate_up[:, start : start + 256]
        for g in range(4):
            for t in range(3):
                at = 1536 * half + 1024 + 128 * g
                feed[16 * t : 16 * t + 16, at : at + 128] = down[16 * g : 16 * g + 16, 128 * t : 128 * t + 128]


def assemble_kernel(
    coords, qkv_own, out_own, up_own, b0, bx, by, bl, bh, d0, dx, dy, dl, dh, w_pairs, w_out, w_up
):
    depth_at, plane_at, core_at = coords[0], coords[1], coords[2]
    w_up[pl.ds(pl.multiple_of(depth_at * 96, 32), 96), :] = up_own[...]
    base = pl.multiple_of(depth_at * 192, 64)
    for part in range(3):
        for p in range(6):
            at = 768 * part + 128 * p
            w_pairs[p, pl.ds(base, 192), 128 * part : 128 * part + 128] = qkv_own[:, at : at + 128]
    w_out[pl.ds(base, 192), :] = out_own[...]
    for core, lows in ((core_at, (b0, bx, by, bl, bh)), (1 - core_at, (d0, dx, dy, dl, dh))):
        column = pl.multiple_of(core * 384, 128)
        tiles = [core * 9 + t for t in range(9)]
        pairs_at = [t % 6 for t in tiles]
        lanes_at = [pl.multiple_of(t // 6 * 128, 128) for t in tiles]
        for far in range(4):
            plane = plane_at ^ far
            for step in range(1, 4):
                shard = (depth_at + step) % 4
                row = pl.multiple_of(shard * 192 + plane * 48, 16)
                if far < 3:
                    left, right = lows[far].at[step - 1, :, 0:1152], lows[far].at[step - 1, :, 1152:1920]
                else:
                    left, right = lows[3].at[step - 1], lows[4].at[step - 1]
                for t in range(9):
                    w_pairs[pairs_at[t], pl.ds(row, 48), pl.ds(lanes_at[t], 128)] = left[:, 128 * t : 128 * t + 128]
                w_out[pl.ds(row, 48), pl.ds(column, 384)] = right[:, 0:384]

                @pl.when(plane < 3)
                def _():
                    for g in range(2):
                        up_row = pl.multiple_of(shard * 96 + plane * 32 + 16 * g, 16)
                        for t in range(3):
                            lane = 384 + 128 * g
                            to = pl.ds(pl.multiple_of(core * 384 + 128 * t, 128), 128)
                            w_up[pl.ds(up_row, 16), to] = right[16 * t : 16 * t + 16, lane : lane + 128]


def lookup_kernel(coords, ids, table_own, t0, tx, ty, tl, th, rows_own, rows_other, table, total):
    plane_at = coords[1]
    at = pl.program_id(0)

    @pl.when(at == 0)
    def _():
        table[...] = table_own[0]
        total[...] = jnp.zeros_like(total)

    for step in range(1, 4):
        @pl.when(at == step)
        def _():
            for far, ref in enumerate((t0, tx, ty)):
                table[pl.ds(pl.multiple_of((plane_at ^ far) * 48, 16), 48), :] = ref[step - 1]
            last = pl.ds(pl.multiple_of((plane_at ^ 3) * 48, 16), 48)
            table[last, 0:896] = tl[step - 1]
            table[last, 896:1792] = th[step - 1]

    wanted = ids[...] - at * 1792
    line = lax.broadcasted_iota(jnp.int32, (256, 1536), 0)
    part = jnp.zeros((192, 1536), F32)
    for chunk in range(7):
        hot = jnp.where(line + 256 * chunk == wanted, 1.0, 0.0).astype(BF16)
        part += mm(table[:, 256 * chunk : 256 * chunk + 256], hot)
    total[...] += part

    @pl.when(at == 3)
    def _():
        rows_own[...] = total[:, 0:768].astype(BF16)
        rows_other[...] = total[:, 768:1536].astype(BF16)


def project_kernel(
    coords, rows_own, rows_other, embedded, w_up, gain, w_pair, cosine, sine,
    residual, act_out, queries, keys, values, act,
):
    core_at = coords[2]

    @pl.when(pl.program_id(0) == 0)
    def _():
        first = pl.multiple_of(core_at * 192, 64)
        second = pl.multiple_of(192 - core_at * 192, 64)
        x = embedded[...].astype(F32)
        x += mm(rows_own[...], w_up[pl.ds(first, 192), :], TN)
        x += mm(rows_other[...], w_up[pl.ds(second, 192), :], TN)
        residual[...] = x
        inverse = lax.rsqrt(jnp.mean(x * x, axis=-1, keepdims=True) + norm_eps)
        low = (x * inverse * gain[...]).astype(BF16)
        act[...] = low
        act_out[...] = low

    projected = mm(act[...], w_pair[0])
    cos, sin = cosine[...], sine[...]
    q, k = projected[:, 0:128], projected[:, 128:256]
    queries[0] = ((q * cos + swap_halves(q) * sin) * 0.125).astype(BF16)
    keys[0] = (k * cos + swap_halves(k) * sin).astype(BF16)
    values[0] = projected[:, 256:384].astype(BF16)


def attend_kernel(last, coords, queries, keys, values, bias, residual, w_out, *rest):
    if last:
        gain, weights_out, attended, middle, act_two, total = rest
    else:
        weights_out, attended, total = rest
    pair = pl.program_id(0)
    lane = lax.broadcasted_iota(jnp.int32, (384, 128), 1)
    columns = []
    for seq in range(2):
        rows = slice(384 * seq, 384 * seq + 384)
        q, k = queries[0, rows, :], keys[0, rows, :]
        v = values[0, rows, :]
        heads = []
        for head in range(2):
            q_head = jnp.where((lane >= 64) == (head == 1), q, jnp.zeros_like(q))
            scores = mm(k, q_head, NT) + bias[seq]
            top = jnp.max(scores, axis=0, keepdims=True)
            raised = jnp.exp(scores - top)
            weight = (raised * (1.0 / jnp.sum(raised, axis=0, keepdims=True))).astype(BF16)
            weights_out[0, seq, head] = weight
            heads.append(mm(weight, jnp.where((lane >= 64) == (head == 1), v, jnp.zeros_like(v)), TN))
        columns.append(heads[0] + heads[1])
    low = jnp.concatenate(columns, axis=0).astype(BF16)
    attended[0] = low
    part = mm(low, w_out[...])

    @pl.when(pair == 0)
    def _():
        total[...] = residual[...] + part

    @pl.when(pair > 0)
    def _():
        total[...] += part

    if not last:
        return

    @pl.when(pair == 2)
    def _():
        mid = total[...]
        middle[...] = mid
        inverse = lax.rsqrt(jnp.mean(mid * mid, axis=-1, keepdims=True) + norm_eps)
        act_two[...] = (mid * inverse * gain[...]).astype(BF16)


def feed_kernel(half, coords, act, cotangent, gate_up_own, down_own, b0, bx, by, bd, d0, dx, dy, dd, *rest):
    if half == 0:
        total, grad_act, grads, w_gate_up, w_down = rest
    else:
        (total_in, grad_act_in, middle, gain, attended_a, attended_b,
         output, grads, grad_mid, grad_low, gain_grad, total, grad_act, w_gate_up, w_down) = rest
    depth_at, plane_at, core_at = coords[0], coords[1], coords[2]
    at = pl.program_id(0)

    def assemble():
        base = pl.multiple_of(depth_at * 192, 64)
        for part in range(2):
            for shard in range(4):
                start = 2048 * part + 512 * shard + 256 * half
                w_gate_up[part, pl.ds(base, 192), 256 * shard : 256 * shard + 256] = gate_up_own[:, start : start + 256]
        w_down[pl.ds(pl.multiple_of(depth_at * 256, 256), 256), :] = down_own[256 * half : 256 * half + 256, :]
        for core, lows in ((core_at, (b0, bx, by, bd)), (1 - core_at, (d0, dx, dy, dd))):
            for far in range(4):
                plane = plane_at ^ far
                for step in range(1, 4):
                    shard = (depth_at + step) % 4
                    row = pl.multiple_of(shard * 192 + plane * 48, 16)
                    piece = lows[far].at[step - 1]
                    w_gate_up[core, pl.ds(row, 48), :] = piece[:, 0:1024]
                    for g in range(4):
                        for t in range(3):
                            row = pl.multiple_of(shard * 256 + plane * 64 + 16 * g, 16)
                            column = pl.multiple_of(core * 384 + 128 * t, 128)
                            lane = 1024 + 128 * g
                            w_down[pl.ds(row, 16), pl.ds(column, 128)] = piece[16 * t : 16 * t + 16, lane : lane + 128]

    @pl.when(at == 0)
    def _():
        total[...] = total_in[...] if half else jnp.zeros_like(total)
        grad_act[...] = grad_act_in[...] if half else jnp.zeros_like(grad_act)
        assemble()

    second = at
    units = pl.ds(pl.multiple_of(second * 512, 512), 512)
    a, c = act[...], cotangent[...]
    w_g, w_u, w_d = w_gate_up[0, :, units], w_gate_up[1, :, units], w_down[units, :]
    gate = mm(a, w_g)
    up = mm(a, w_u)
    back = mm(c, w_d, NT)
    sig = 0.5 * jnp.tanh(0.5 * gate) + 0.5
    silu = gate * sig
    inner = (silu * up).astype(BF16)
    d_up = (back * silu).astype(BF16)
    d_gate = (back * up * (sig * (1.0 + gate * (1.0 - sig)))).astype(BF16)
    total[...] += mm(inner, w_d)
    grad_act[...] += mm(d_gate, w_g, NT) + mm(d_up, w_u, NT)
    gate_g = mm(a, d_gate, TN).astype(BF16)
    up_g = mm(a, d_up, TN).astype(BF16)
    down = mm(inner, c, TN).astype(BF16)
    lanes = pl.ds(pl.multiple_of(second * 512, 512), 512)
    for plane in range(4):
        for core in range(2):
            q = 2 * plane + core
            block = up_g if core else gate_g
            for shard in range(4):
                row = 192 * shard + 48 * plane
                grads[q, (shard + 4 - depth_at) % 4, :, lanes] = block[row : row + 48, :]
            for b in range(2):
                for g in range(4):
                    low_lanes = slice(1024 + 128 * g, 1152 + 128 * g)
                    for t in range(3):
                        row = 256 * b + 64 * plane + 16 * g
                        column = 384 * core + 128 * t
                        grads[q, (2 * second + b + 4 - depth_at) % 4, 16 * t : 16 * t + 16, low_lanes] = down[
                            row : row + 16, column : column + 128
                        ]

    if half == 0:
        return

    @pl.when(at == 1)
    def _():
        mid = middle[...]
        output[...] = (mid + total[...]).astype(BF16)
        inverse = lax.rsqrt(jnp.mean(mid * mid, axis=-1, keepdims=True) + norm_eps)
        normed = mid * inverse
        grad = grad_act[...]
        gain_grad[...] = jnp.sum(grad * normed, axis=0, keepdims=True)
        n = grad * gain[...]
        g = cotangent[...].astype(F32) + inverse * (n - normed * jnp.mean(n * normed, axis=-1, keepdims=True))
        grad_mid[...] = g
        low = g.astype(BF16)
        grad_low[...] = low
        out_g = [mm(attended[p], low, TN) for attended in (attended_a, attended_b) for p in range(3)]
        out_g = jnp.concatenate(out_g, axis=0).astype(BF16)
        for plane in range(4):
            for core in range(2):
                for shard in range(4):
                    row = 192 * shard + 48 * plane
                    grads[2 * plane + core, (shard + 4 - depth_at) % 4, :, 1536:1920] = out_g[row : row + 48, 384 * core : 384 * core + 384]


def second_half_kernel(
    coords, queries, keys, values, weights_a, weights_b, grad_low, w_out, w_pair, cosine, sine,
    w_up, residual, grad_mid, gain,
    embedding_grad, grad_projected, rows_kept, rows_sent, gain_grad, grad_act,
):
    depth_at, plane_at, core_at = coords[0], coords[1], coords[2]
    step = pl.program_id(0)
    lane = lax.broadcasted_iota(jnp.int32, (384, 128), 1)

    @pl.when(step == 0)
    def _():
        grad_act[...] = jnp.zeros_like(grad_act)

    grad_attended = mm(grad_low[...], w_out[...], NT).astype(BF16)
    threes = []
    for seq in range(2):
        rows = slice(384 * seq, 384 * seq + 384)
        q, k, v, ga = queries[0, rows, :], keys[0, rows, :], values[0, rows, :], grad_attended[rows, :]
        grad_q = jnp.zeros((384, 128), F32)
        grad_k = jnp.zeros((384, 128), F32)
        grad_v = jnp.zeros((384, 128), F32)
        for head in range(2):
            mine = (lane >= 64) == (head == 1)
            ga_head = jnp.where(mine, ga, jnp.zeros_like(ga))
            q_head = jnp.where(mine, q, jnp.zeros_like(q))
            weight_low = jnp.where(step < 3, weights_a[0, seq, head], weights_b[0, seq, head])
            weight = weight_low.astype(F32)
            grad_weight = mm(v, ga_head, NT)
            row = jnp.sum(grad_weight * weight, axis=0, keepdims=True)
            grad_scores = (weight * (grad_weight - row)).astype(BF16)
            grad_v += mm(weight_low, ga_head)
            grad_k += mm(grad_scores, q_head)
            grad_q += mm(grad_scores, jnp.where(mine, k, jnp.zeros_like(k)), TN)
        grad_q = grad_q * 0.125
        cos, sin = cosine[rows, :], sine[rows, :]
        grad_q = (grad_q * cos - swap_halves(grad_q) * sin).astype(BF16)
        grad_k = (grad_k * cos - swap_halves(grad_k) * sin).astype(BF16)
        threes.append(jnp.concatenate([grad_q, grad_k, grad_v.astype(BF16)], axis=1))
    three = jnp.concatenate(threes, axis=0)
    grad_act[...] += mm(three, w_pair[0], NT)
    grad_projected[0] = three

    @pl.when(step == 5)
    def _():
        grad = grad_act[...]
        x = residual[...]
        inverse = lax.rsqrt(jnp.mean(x * x, axis=-1, keepdims=True) + norm_eps)
        normed = x * inverse
        gain_grad[...] = jnp.sum(grad * normed, axis=0, keepdims=True)
        n = grad * gain[...]
        g = grad_mid[...] + inverse * (n - normed * jnp.mean(n * normed, axis=-1, keepdims=True))
        low = g.astype(BF16)
        embedding_grad[...] = low
        rows = mm(w_up[...], low, NT).astype(BF16)

        @pl.when(core_at == 0)
        def _():
            rows_kept[...] = rows[0:192]
            rows_sent[...] = rows[192:384]

        @pl.when(core_at == 1)
        def _():
            rows_kept[...] = rows[192:384]
            rows_sent[...] = rows[0:192]


def both_ways(core_at, kept, sent, place):
    @pl.when(core_at == 0)
    def _():
        place(0, kept)
        place(1, sent)

    @pl.when(core_at == 1)
    def _():
        place(1, kept)
        place(0, sent)


def weight_grad_kernel(coords, act, grad_projected, kept, sent):
    depth_at, plane_at, core_at = coords[0], coords[1], coords[2]
    step = pl.program_id(0)
    weight_g = mm(act[...], grad_projected[0], TN)

    def place(core, out):
        for part in range(3):
            lanes = pl.ds(pl.multiple_of(512 + 768 * part + step * 128, 128), 128)
            for plane in range(4):
                for shard in range(4):
                    row = 192 * shard + 96 * core + 24 * plane
                    out[(shard + 4 - depth_at) % 4, plane ^ plane_at, :, lanes] = weight_g[
                        row : row + 24, 128 * part : 128 * part + 128
                    ].astype(BF16)

    both_ways(core_at, kept, sent, place)


def up_grad_kernel(
    coords, kept_in, sent_in, rows_own, rows_other, embedding_grad, gain_one_grad, gain_two_grad, kept, sent
):
    depth_at, plane_at, core_at = coords[0], coords[1], coords[2]
    low = embedding_grad[...]
    mine, other = mm(rows_own[...], low), mm(rows_other[...], low)
    first = jnp.where(core_at == 0, mine, other)
    second = jnp.where(core_at == 0, other, mine)
    both = jnp.concatenate([first, second], axis=0)
    one, two = gain_one_grad[...], gain_two_grad[...]

    def place(core, out):
        for plane in range(4):
            for shard in range(4):
                row = 96 * shard + 24 * plane
                far, near = (shard + 4 - depth_at) % 4, plane ^ plane_at
                out[far, near, :, 0:384] = both[row : row + 24, 384 * core : 384 * core + 384].astype(BF16)
                lines = jnp.zeros((24, 128), F32)
                if core == 0 and plane == 0:
                    start = 192 * shard
                    line = jnp.concatenate([one[:, start : start + 192], two[:, start : start + 192]], axis=1)
                    lines = jnp.concatenate(
                        [line[:, 0:128], line[:, 128:256], line[:, 256:384], jnp.zeros((21, 128), F32)], axis=0
                    )
                out[far, near, :, 384:512] = lines.astype(BF16)

    both_ways(core_at, kept, sent, place)


def table_add(ids, ref, total):
    line = lax.broadcasted_iota(jnp.int32, (2048, 768), 0)
    hot = jnp.where(line == ids[0], 1.0, 0.0).astype(BF16)
    total[...] += mm(ref[0] if len(ref.shape) == 3 else ref[...], hot, NT)


def table_kernel(sources, first, coords, ids, *rest):
    refs = rest[:sources]
    total = rest[-1]
    at = pl.program_id(0)

    @pl.when(at == 0)
    def _():
        total[...] = jnp.zeros_like(total) if first else rest[sources][...]

    for source, ref in enumerate(refs):
        @pl.when(at == source)
        def _():
            table_add(ids, ref, total)


def table_last_kernel(coords, ids, low, high, before, kept_x, kept_y, got_y, got_x, *rest):
    outs, total = rest[:4], rest[4]
    at = pl.program_id(0)

    @pl.when(at == 0)
    def _():
        total[...] = before[...]
        table_add(ids, low, total)
        for i in range(2):
            outs[i][:, 0:2816] = (kept_x[i].astype(F32) + got_y[i].astype(F32)).astype(BF16)
            outs[i + 2][:, 0:2816] = (kept_y[i].astype(F32) + got_x[i].astype(F32)).astype(BF16)

    @pl.when(at == 1)
    def _():
        table_add(ids, high, total)
        for shard in range(4):
            for g in range(8):
                lane = 2816 + 512 * g
                outs[shard][:, lane : lane + 512] = total[24 * g : 24 * g + 24, 512 * shard : 512 * shard + 512].astype(BF16)


def add_kernel(coords, *refs):
    total = refs[0][...].astype(F32)
    for ref in refs[1:-1]:
        total = total + ref[...].astype(F32)
    refs[-1][...] = total.astype(BF16)


def join_kernel(coords, first, *refs):
    refs[-1][:, 0:1536] = first[...]
    total = refs[0][...].astype(F32)
    for ref in refs[1:-1]:
        total = total + ref[...].astype(F32)
    refs[-1][:, 1536:3456] = total.astype(BF16)


def add_all(coords, parts, after=()):
    shape = parts[0].shape
    return kernel_call(
        add_kernel, coords, parts, [full(shape)] * len(parts), [sds(shape, BF16)], [full(shape)], (1,),
        micros=1.5, vmem=16, name="add", after=after,
    )[0]


def split_kernel(coords, value, *parts):
    for at, part in enumerate(parts):
        part[...] = value[0, at]


def first_sum_kernel(coords, kept, got, send_x, send_y, keep_x, keep_y):
    for shard in range(4):
        for plane in range(4):
            value = (kept[shard, plane].astype(F32) + got[shard, plane].astype(F32)).astype(BF16)
            if shard < 2:
                (send_x if plane % 2 else keep_x)[shard, plane // 2] = value
            else:
                (send_y if plane // 2 else keep_y)[shard - 2, plane % 2] = value


def second_sum_kernel(coords, keep_x, keep_y, got_x, got_y, send_y, send_x, kept_x, kept_y):
    for i in range(2):
        send_y[i] = (keep_x[i, 1].astype(F32) + got_x[i, 1].astype(F32)).astype(BF16)
        send_x[i] = (keep_y[i, 1].astype(F32) + got_y[i, 1].astype(F32)).astype(BF16)
        kept_x[i] = (keep_x[i, 0].astype(F32) + got_x[i, 0].astype(F32)).astype(BF16)
        kept_y[i] = (keep_y[i, 0].astype(F32) + got_y[i, 0].astype(F32)).astype(BF16)


def each_piece(coords, refs):
    for index, ref in enumerate(refs):
        yield coords[2] ^ (index // 4), coords[1] ^ (index % 4), ref


def finish_feed_kernel(coords, *refs):
    gate_up, down, out = refs[8:]
    for core, plane, ref in each_piece(coords, refs[0:8]):
        rows = pl.ds(pl.multiple_of(plane * 48, 16), 48)
        for half in range(2):
            for j in range(4):
                lanes = pl.ds(pl.multiple_of(core * 2048 + 512 * j + 256 * half, 256), 256)
                at = 1536 * half + 256 * j
                gate_up[rows, lanes] = ref[:, at : at + 256].astype(F32)
            for g in range(4):
                for t in range(3):
                    low_rows = pl.ds(pl.multiple_of(256 * half + plane * 64 + 16 * g, 16), 16)
                    lanes = pl.ds(pl.multiple_of(core * 384 + 128 * t, 128), 128)
                    at = 1536 * half + 1024 + 128 * g
                    down[low_rows, lanes] = ref[16 * t : 16 * t + 16, at : at + 128].astype(F32)
        out[rows, pl.ds(pl.multiple_of(core * 384, 128), 384)] = ref[:, 3072:3456].astype(F32)


def finish_rest_kernel(coords, *refs):
    qkv, up, gains, table = refs[8:]
    for core, plane, ref in each_piece(coords, refs[0:8]):
        rows = pl.ds(pl.multiple_of(core * 96 + plane * 24, 8), 24)
        qkv[rows, :] = ref[:, 512:2816].astype(F32)
        up_rows = pl.ds(pl.multiple_of(plane * 24, 8), 24)
        up[up_rows, pl.ds(pl.multiple_of(core * 384, 128), 384)] = ref[:, 0:384].astype(F32)
        for g in range(8):
            lane = 2816 + 512 * g
            at = pl.ds(pl.multiple_of(plane * 512, 512), 256)
            table[core, 24 * g : 24 * g + 24, at] = ref[:, lane : lane + 256].astype(F32)

        @pl.when(plane < 3)
        def _():
            for g in range(8):
                lane = 2816 + 512 * g + 256
                at = pl.ds(pl.multiple_of(plane * 512 + 256, 256), 256)
                table[core, 24 * g : 24 * g + 24, at] = ref[:, lane : lane + 256].astype(F32)

        @pl.when((core == 0) & (plane == 0))
        def _():
            value = ref[:, 384:512].astype(F32)
            line = jnp.concatenate([value[i : i + 1] for i in range(3)], axis=1)
            gains[0:1, :] = line[:, 0:192]
            gains[1:2, :] = line[:, 192:384]


def rotary_lanes(segments):
    seq_len = segments.shape[-1]
    position = jnp.arange(seq_len, dtype=jnp.int32)
    same = segments[:, :, None] == segments[:, None, :]
    start = jnp.min(jnp.where(same, position[None, None, :], seq_len), axis=-1)
    offset = (position[None, :] - start).astype(F32)
    half = HEAD_DIM // 2
    frequency = theta_base ** (-jnp.arange(half, dtype=F32) / half)
    angle = offset[..., None] * frequency
    cos, sin = jnp.cos(angle), jnp.sin(angle)
    cosine = jnp.concatenate([cos, cos, cos, cos], axis=-1)
    sine = jnp.concatenate([-sin, sin, -sin, sin], axis=-1)
    return cosine.reshape(-1, 128), sine.reshape(-1, 128), same


def body(
    sizes, embedded, cotangent, ngram_ids, segments, live_mask, tables, w_qkv, w_out, w_gate_up, w_down, up_proj, norm_gains
):
    depth, groups = sizes
    micro, _, seq, width = embedded.shape
    tokens = micro * seq
    rows_dev = tables.shape[1]
    depth_at = lax.axis_index("fsdp")
    octet = lax.axis_index("oct")
    core_at = octet & 1
    plane_at = octet >> 1
    coords = jnp.stack([depth_at, plane_at, core_at]).astype(jnp.int32)
    embedded = embedded.reshape(tokens, width)
    cotangent = cotangent.reshape(tokens, width)
    segments = segments.reshape(micro, seq)
    live_mask = live_mask.reshape(micro, seq)
    ids = ngram_ids.reshape(2, tokens)
    tables_t = jnp.transpose(tables, (0, 2, 1))

    gain_block = jnp.pad(norm_gains.reshape(3, 128), ((0, 45), (0, 0)))
    (top,) = kernel_call(
        prepare_table_kernel,
        coords,
        [tables_t],
        [pl.BlockSpec((1, 48, rows_dev), lambda i, at: (at[2], at[1], 0))],
        [sds((48, rows_dev), BF16)],
        [full((48, rows_dev))],
        (1,),
        micros=1,
        name="prepare_table",
    )
    top_held = stack(coords, along_depth(top, depth))
    top_x, top_y = by_x(top_held), by_y(top_held)
    (low,) = kernel_call(
        prepare_low_kernel,
        coords,
        [w_qkv, w_out, up_proj, gain_block],
        [
            pl.BlockSpec((48, 1152), lambda i, at: (at[1], at[2])),
            pl.BlockSpec((48, 384), lambda i, at: (at[1], at[2])),
            pl.BlockSpec((32, 384), lambda i, at: (jnp.minimum(at[1], 2), at[2])),
            full((48, 128)),
        ],
        [sds((48, 1920), BF16)],
        [full((48, 1920))],
        (1,),
        micros=1,
        name="prepare_low",
        after=[top_held],
    )
    low_steps = along_depth(low, depth)
    top_low, top_high = cut_pieces(coords, top_x, top_y, 896)
    low_held = stack(coords, low_steps, after=[top_low])
    low_x, low_y = by_x(low_held), by_y(low_held)
    tops = [top_held, top_x, top_y, by_y(top_low), by_x(top_high)]
    (feed,) = kernel_call(
        prepare_feed_kernel,
        coords,
        [w_gate_up, w_down, w_down],
        [
            pl.BlockSpec((48, 2048), lambda i, at: (at[1], at[2])),
            pl.BlockSpec((64, 384), lambda i, at: (at[1], at[2])),
            pl.BlockSpec((64, 384), lambda i, at: (4 + at[1], at[2])),
        ],
        [sds((48, 3072), BF16)],
        [full((48, 3072))],
        (1,),
        micros=1,
        name="prepare_feed",
        after=[low_held],
    )

    feed_steps = along_depth(feed, depth)

    gains_rel = jnp.concatenate([norm_gains[None], low_held[:, 0:3, 1792:1920].reshape(depth - 1, 2, 192)], axis=0)
    gains = jnp.roll(gains_rel, depth_at, axis=0).transpose(1, 0, 2).reshape(2, width).astype(F32)
    gain_one, gain_two = gains[0:1], gains[1:2]

    ids_other = by_core(ids)
    wanted = jnp.concatenate(
        [
            lax.dynamic_index_in_dim(ids, core_at, axis=0),
            lax.dynamic_index_in_dim(ids_other, core_at, axis=0),
        ],
        axis=0,
    )
    shard = wanted // rows_dev
    inside = wanted - shard * rows_dev
    line = ((shard - depth_at) % depth) * rows_dev + inside
    rows_own, rows_sent = kernel_call(
        lookup_kernel,
        coords,
        [line.reshape(1, 2 * tokens), tables_t] + list(tops),
        [full((1, 2 * tokens)), pl.BlockSpec((1, 192, rows_dev), lambda i, at: (at[2], 0, 0))] + [full(t.shape) for t in tops],
        [sds((192, tokens), BF16)] * 2,
        [full((192, tokens))] * 2,
        (4,),
        scratch=[pltpu.VMEM((192, rows_dev), BF16), pltpu.VMEM((192, 2 * tokens), F32)],
        micros=8,
        name="lookup",
        after=[low_held, feed],
    )
    rows_other = by_core(rows_sent)

    low_low, low_high = cut_pieces(coords, low_x, low_y, 1152, after=[rows_sent])
    lows = [low_held, low_x, low_y, by_y(low_low), by_x(low_high)]
    gathered = lows + [by_core(piece) for piece in lows]
    feed_held = stack(coords, feed_steps, after=[low_low])
    feed_x, feed_y = by_x(feed_held), by_y(feed_held)
    w_pairs, w_out_full, w_up_full = kernel_call(
        assemble_kernel,
        coords,
        [w_qkv, w_out, up_proj] + gathered,
        [full(a.shape) for a in [w_qkv, w_out, up_proj] + gathered],
        [sds((6, width, 384), BF16), sds((width, width), BF16), sds((384, width), BF16)],
        [full((6, width, 384)), full((width, width)), full((384, width))],
        (1,),
        vmem=60,
        name="assemble",
        after=[feed_held],
    )

    near = jnp.stack([wanted, by_x(wanted)])
    plane_ids = jnp.concatenate([near, by_y(near)], axis=0)
    t_shard = plane_ids // rows_dev
    t_inside = plane_ids - t_shard * rows_dev
    target = jnp.where(
        t_inside // 512 == plane_at, ((t_shard - depth_at) % depth) * 512 + t_inside % 512, -1
    ).reshape(8, 1, tokens)

    cosine, sine, same = rotary_lanes(segments)
    position = jnp.arange(seq, dtype=jnp.int32)
    usable = same & (position[None, :, None] <= position[None, None, :]) & (live_mask[:, :, None] == 1)
    usable = usable | (position[None, :, None] == position[None, None, :])
    bias = jnp.where(usable, 0.0, masked_score).astype(F32)

    whole = full((tokens, width))
    line_spec = full((1, width))
    turn = full((tokens, 128))

    def pair_block(start):
        return pl.BlockSpec((1, tokens, 128), lambda p, *_: (p + start, 0, 0))

    residual, act_one, queries, keys, values = kernel_call(
        project_kernel,
        coords,
        [rows_own, rows_other, embedded, w_up_full, gain_one, w_pairs, cosine, sine],
        [full((192, tokens))] * 2
        + [whole, full((384, width)), line_spec, pl.BlockSpec((1, width, 384), lambda p, *_: (p, 0, 0)), turn, turn],
        [sds((tokens, width), F32), sds((tokens, width), BF16)] + [sds((6, tokens, 128), BF16)] * 3,
        [whole, whole] + [pair_block(0)] * 3,
        (6,),
        scratch=[pltpu.VMEM((tokens, width), BF16)],
        micros=12,
        vmem=36,
        name="project",
        after=[target],
    )

    def attend_call(start, before, extra, extra_specs, outs, out_specs, after):
        return kernel_call(
            lambda *refs: attend_kernel(start > 0, *refs),
            coords,
            [queries, keys, values, bias, before, w_out_full] + extra,
            [pair_block(start)] * 3
            + [full((micro, seq, seq)), whole, pl.BlockSpec((128, width), lambda p, *_: (p + start, 0))] + extra_specs,
            [sds((3, micro, 2, seq, seq), BF16), sds((3, tokens, 128), BF16)] + outs,
            [pl.BlockSpec((1, micro, 2, seq, seq), lambda p, *_: (p, 0, 0, 0, 0)),
             pair_block(0)] + out_specs,
            (3,),
            scratch=[pltpu.VMEM((tokens, width), F32)] if start else [],
            micros=12,
            name="attend",
            after=after,
        )

    feed_low, feed_high = cut_pieces(coords, feed_x, feed_y, 1536, after=[queries])
    feed_low, feed_high = by_y(feed_low), by_x(feed_high)
    weights_a, attended_a, partial = attend_call(0, residual, [], [], [sds((tokens, width), F32)], [whole], [])
    weights_b, attended_b, middle, act_two = attend_call(
        3, partial, [gain_two], [line_spec],
        [sds((tokens, width), F32), sds((tokens, width), BF16)], [whole, whole],
        [feed_low, feed_high],
    )
    wholes = [feed_held, feed_x, feed_y]
    others = [by_core(piece) for piece in wholes]
    feed_parts = [wholes + [feed_low] + others + [by_core(feed_low)], wholes + [feed_high] + others + [by_core(feed_high)]]

    def single(shape):
        return pl.BlockSpec(shape, lambda *_: (0,) * len(shape), pipeline_mode=pl.Buffered(1))

    one = single((tokens, width))
    feed_scratch = [pltpu.VMEM((2, width, 1024), BF16), pltpu.VMEM((1024, width), BF16)]

    def feed_specs(half):
        part = pl.BlockSpec((depth - 1, 48, 1536), lambda *_: (0, 0, half), pipeline_mode=pl.Buffered(1))
        return [one, one, single(w_gate_up.shape), single(w_down.shape)] + ([part] * 3 + [single((depth - 1, 48, 1536))]) * 2

    feed_in = [act_two, cotangent, w_gate_up, w_down]
    grads_shapes = [(8, depth, 48, 1536), (8, depth, 48, 1920)]
    total, grad_act, feed_grads = kernel_call(
        lambda *refs: feed_kernel(0, *refs),
        coords,
        feed_in + feed_parts[0],
        feed_specs(0),
        [sds((tokens, width), F32), sds((tokens, width), F32), sds(grads_shapes[0], BF16)],
        [one, one, single(grads_shapes[0])],
        (2,),
        scratch=feed_scratch,
        micros=20,
        vmem=54,
        name="feed_first",
    )
    feed_part_a = lax.psum_scatter(feed_grads, "oct", scatter_dimension=0, tiled=True)
    output, feed_grads, grad_mid, grad_low, gain_two_grad = kernel_call(
        lambda *refs: feed_kernel(1, *refs),
        coords,
        feed_in + feed_parts[1] + [total, grad_act, middle, gain_two, attended_a, attended_b],
        feed_specs(1) + [one, one, one, line_spec] + [single((3, tokens, 128))] * 2,
        [sds((tokens, width), BF16), sds(grads_shapes[1], BF16), sds((tokens, width), F32), sds((tokens, width), BF16),
         sds((1, width), F32)],
        [one, single(grads_shapes[1]), one, one, line_spec],
        (2,),
        scratch=[pltpu.VMEM((tokens, width), F32)] * 2 + feed_scratch,
        micros=24,
        vmem=54,
        name="feed_second",
    )
    feed_part_b = lax.psum_scatter(feed_grads, "oct", scatter_dimension=0, tiled=True)

    def steps_block(shape, place):
        return pl.BlockSpec(shape, lambda p, *_: place(p) + (0,) * (len(shape) - 1))

    tail_shape = sds((4, 4, 24, 2816), BF16)
    weights_shape = (1, micro, 2, seq, seq)
    embedding_grad, grad_projected, rows_kept, rows_sent, gain_one_grad = kernel_call(
        second_half_kernel,
        coords,
        [queries, keys, values, weights_a, weights_b, grad_low, w_out_full, w_pairs, cosine, sine, w_up_full, residual,
         grad_mid, gain_one],
        [pair_block(0)] * 3
        + [steps_block(weights_shape, lambda p: (jnp.minimum(p, 2),)), steps_block(weights_shape, lambda p: (jnp.maximum(p - 3, 0),)),
           whole, pl.BlockSpec((128, width), lambda p, *_: (p, 0)), pl.BlockSpec((1, width, 384), lambda p, *_: (p, 0, 0)),
           turn, turn, full((384, width)), whole, whole, line_spec],
        [sds((tokens, width), BF16), sds((6, tokens, 384), BF16), sds((192, tokens), BF16), sds((192, tokens), BF16),
         sds((1, width), F32)],
        [whole, pl.BlockSpec((1, tokens, 384), lambda p, *_: (p, 0, 0)), full((192, tokens)), full((192, tokens)), line_spec],
        (6,),
        scratch=[pltpu.VMEM((tokens, width), F32)],
        micros=36,
        name="second_half",
    )

    rows_got = by_core(rows_sent)
    held = stack(coords, [rows_kept, rows_got])
    held_x, held_y = by_x(held), by_y(held)
    kept_c, sent_c = kernel_call(
        weight_grad_kernel,
        coords,
        [act_one, grad_projected],
        [whole, pl.BlockSpec((1, tokens, 384), lambda p, *_: (p, 0, 0))],
        [tail_shape, tail_shape],
        [full(tail_shape.shape)] * 2,
        (6,),
        micros=9,
        name="weight_grad",
        after=[held],
    )

    def split_call(part, after):
        shape = part.shape[2:]
        shards = kernel_call(
            split_kernel, coords, [part], [full(part.shape)], [sds(shape, BF16)] * depth, [full(shape)] * depth,
            (1,), micros=2, vmem=16, name="split", after=after,
        )
        return [shards[0]] + [to_ahead(shards[step], step, depth) for step in range(1, depth)]

    held_low, held_high = held_x[0], held_y[1]
    up_block = pl.BlockSpec((4, 4, 24, 512), lambda *_: (0, 0, 0, 0))
    kept_c, sent_c = kernel_call(
        up_grad_kernel,
        coords,
        [kept_c, sent_c, rows_own, rows_other, embedding_grad, gain_one_grad, gain_two_grad],
        [pl.BlockSpec(memory_space=pl.ANY)] * 2
        + [full((192, tokens)), full((192, tokens)), whole, line_spec, line_spec],
        [tail_shape, tail_shape],
        [up_block, up_block],
        (1,),
        micros=3,
        vmem=24,
        name="up_grad",
        after=[held_low, held_high],
        aliases=[(0, 0), (1, 1)],
    )
    held_low, held_high = by_y(held_low), by_x(held_high)
    got_c = by_core(sent_c)

    part_shape, low_shape = (2, 2, 24, 2816), (2, 24, 2816)
    send_x, send_y, keep_x, keep_y = kernel_call(
        first_sum_kernel, coords, [kept_c, got_c], [full(tail_shape.shape)] * 2, [sds(part_shape, BF16)] * 4,
        [full(part_shape)] * 4, (1,), micros=3, vmem=24, name="first_sum",
    )
    c_x, c_y = by_x(send_x), by_y(send_y)
    feed_got_a = split_call(feed_part_a, [send_x])

    def table_call(sources, refs, places, before, after):
        specs = [pl.BlockSpec((1, 192, tokens), lambda i, *_, place=place: (place, 0, 0)) for place in places]
        return kernel_call(
            lambda *r: table_kernel(len(refs), before is None, *r),
            coords,
            [target[sources]] + refs + ([] if before is None else [before]),
            [pl.BlockSpec((1, 1, tokens), lambda i, *_: (i, 0, 0))] + specs + ([] if before is None else [full((192, 2048))]),
            [sds((192, 2048), F32)],
            [full((192, 2048))],
            (len(refs),),
            micros=3 + len(refs),
            vmem=24,
        name="table_sum",
            after=after,
        )[0]

    sums = table_call(slice(0, 2), [held, held], [0, 1], None, [send_x])
    feed_sum_a = add_all(coords, feed_got_a, [send_x])
    send_y, send_x, kept_x, kept_y = kernel_call(
        second_sum_kernel, coords, [keep_x, keep_y, c_x, c_y], [full(part_shape)] * 4, [sds(low_shape, BF16)] * 4,
        [full(low_shape)] * 4, (1,), micros=2, vmem=16, name="second_sum", after=[feed_sum_a],
    )
    c_y, c_x = by_y(send_y), by_x(send_x)
    feed_got_b = split_call(feed_part_b, [send_y])
    sums = table_call(slice(2, 6), [held_x, held_x, held_y, held_y], [0, 1, 0, 1], sums, [feed_got_b[0]])
    shard_shape = (24, 6912)
    shards = kernel_call(
        table_last_kernel,
        coords,
        [target[6:8], held_low, held_high, sums, kept_x, kept_y, c_y, c_x],
        [pl.BlockSpec((1, 1, tokens), lambda i, *_: (i, 0, 0))] + [full((192, tokens))] * 2 + [full((192, 2048))]
        + [full(low_shape)] * 4,
        [sds(shard_shape, BF16)] * 4,
        [full(shard_shape)] * 4,
        (2,),
        scratch=[pltpu.VMEM((192, 2048), F32)],
        micros=6,
        vmem=24,
        name="table_last",
    )
    tail_got = [shards[0]] + [to_ahead(shards[step], step, depth) for step in range(1, depth)]
    pieces = spread(over_groups(add_all(coords, tail_got), groups))
    feed_sum = kernel_call(
        join_kernel, coords, [feed_sum_a] + feed_got_b, [full((48, 1536))] + [full((48, 1920))] * 4, [sds((48, 3456), BF16)],
        [full((48, 3456))], (1,), micros=2, vmem=16, name="join",
    )[0]
    feed_pieces = spread(over_groups(feed_sum, groups))

    def finish(kernel, refs, outs, name):
        return kernel_call(
            kernel, coords, refs, [full(r.shape) for r in refs], outs, [full(o.shape) for o in outs], (1,), vmem=32, name=name
        )

    gate_up_grad, down_grad, out_grad = finish(
        finish_feed_kernel,
        feed_pieces,
        [sds((192, 4096), F32), sds((512, width), F32), sds((192, width), F32)],
        "finish_feed",
    )
    qkv_grad, up_grad, gains_grad, table_grad = finish(
        finish_rest_kernel,
        pieces,
        [sds((192, 2304), F32), sds((96, width), F32), sds((2, 192), F32), sds((2, 192, rows_dev), F32)],
        "finish_rest",
    )
    return (
        output.reshape(micro, 1, seq, width),
        embedding_grad.reshape(micro, 1, seq, width),
        jnp.transpose(table_grad, (0, 2, 1)),
        qkv_grad,
        out_grad,
        gate_up_grad,
        down_grad,
        up_grad,
        gains_grad,
    )


def solution(mesh):
    depth, rep = mesh.devices.shape
    groups = rep // 8
    fine = Mesh(mesh.devices.reshape(depth, groups, 8), ("fsdp", "grp", "oct"))
    every = ("fsdp", "grp", "oct")
    in_specs = (
        P(None, every, None, None),
        P(None, every, None, None),
        P(None, None, every, None),
        P(None, every, None),
        P(None, every, None),
        P(None, "fsdp", None),
        P("fsdp", None),
        P("fsdp", None),
        P("fsdp", None),
        P("fsdp", None),
        P("fsdp", None),
        P(None, "fsdp"),
    )
    out_specs = (
        P(None, every, None, None),
        P(None, every, None, None),
        P(None, "fsdp", None),
        P("fsdp", None),
        P("fsdp", None),
        P("fsdp", None),
        P("fsdp", None),
        P("fsdp", None),
        P(None, "fsdp"),
    )

    def step(*args):
        return body((depth, groups), *args)

    return jax.shard_map(step, mesh=fine, in_specs=in_specs, out_specs=out_specs, check_vma=False)
```
